512 devices in a mesh: ta: 8 (over z), ha: 8 (over y), wa: 8 (over x, core).
Axes of the slice: x: 4, y: 8, z: 8, core: 2. Of those that a mesh axis runs over, the one named last changes fastest.
Arguments:
- features: float32 [16, 64, 128, 256], P('ta', 'ha', 'wa'), may hold values from -40 to 40
- cotangent: float32 [16, 64, 128, 256], P('ta', 'ha', 'wa'), may hold values from -6 to 6
- conv_one: bfloat16 [3, 2304, 256], P(None, ('ha', 'wa')), may hold values from -0.078125 to 0.078125
- conv_two: bfloat16 [3, 2304, 256], P(None, ('ha', 'wa')), may hold values from -0.078125 to 0.078125
- gain_one: float32 [256], replicated, may hold values from 0.25 to 1.75
- bias_one: float32 [256], replicated, may hold values from -3 to 3
- gain_two: float32 [256], replicated, may hold values from 0.25 to 1.75
- bias_two: float32 [256], replicated, may hold values from -3 to 3
Outputs:
- block_out: float32 [16, 64, 128, 256], P('ta', 'ha', 'wa')
- grad_input: float32 [16, 64, 128, 256], P('ta', 'ha', 'wa')
- norm_grads: float32 [4, 256], replicated
The draws below stay inside these ranges and needn't reach their ends.
All inputs are finite; a program needn't handle non-finite values.
Results may differ from the reference program's by a relative error of at most 0.0041.
Values may be sent and summed in bfloat16 or wider, within the bound.
A program may use at most 64 MiB of HBM per device.

```python
import jax
import jax.numpy as jnp
from jax import lax

C = 256
GROUPS = 32
NT = 16
NH = 64
NW = 128


def draw_features(key, part):
    key = jax.random.fold_in(key, 11)
    key_noise, key_rough, key_offset = jax.random.split(key, 3)
    shape = (NT, NH, NW, C)
    pos_time = jnp.arange(NT, dtype=jnp.float32)[:, None, None, None] / NT
    pos_height = jnp.arange(NH, dtype=jnp.float32)[None, :, None, None] / NH
    pos_width = jnp.arange(NW, dtype=jnp.float32)[None, None, :, None] / NW
    scale = jnp.exp(jnp.log(3.0) * (pos_time + pos_height + pos_width) / 2.0)
    noise = jax.random.truncated_normal(key_noise, -4.0, 4.0, shape, jnp.float32)
    rough = jax.random.uniform(key_rough, shape, jnp.float32, 0.5, 1.5)
    offset = 0.5 * jax.random.truncated_normal(key_offset, -3.0, 3.0, (C,), jnp.float32)
    return (noise * rough * scale + offset).astype(jnp.float32)


def block_levels(rng, shape, shards, smallest, top_value):
    factor_of, own = 1.0, jax.random.fold_in(rng, 6)
    for position, shards_of in shards:
        heights = jnp.exp(jax.random.uniform(jax.random.fold_in(own, position), (shards_of,), jnp.float32, smallest / len(shards), top_value / len(shards)))
        factor_of = factor_of * jnp.repeat(heights, shape[position] // shards_of).reshape([-1 if axis == position else 1 for axis in range(len(shape))])
    return factor_of


def scatter_about(own_key, extent, scale, limit, cuts=(), kind=jnp.bfloat16):
    drawn = scale * jax.random.normal(own_key, extent, jnp.float32)
    if cuts:
        drawn = drawn * block_levels(own_key, extent, cuts, -0.22, 0.18)
    return jnp.clip(drawn, -limit, limit).astype(kind)


def setup_inputs(seed: int = 0) -> dict:
    key_of = jax.random.split(jax.random.key(seed), 9)
    return {
        "features": draw_features(jax.random.fold_in(key_of[8], 71), 0),
        "cotangent": scatter_about(key_of[1], (NT, NH, NW, C), 1.0, 6.0, ((0, 8), (1, 8), (2, 8)), jnp.float32),
        "conv_one": scatter_about(key_of[2], (3, 9 * C, C), (27 * C) ** -0.5, 0.078125, ((1, 64),)),
        "conv_two": scatter_about(key_of[3], (3, 9 * C, C), (27 * C) ** -0.5, 0.078125, ((1, 64),)),
        "gain_one": jnp.clip(1.0 + 0.15 * jax.random.normal(key_of[4], (C,), jnp.float32), 0.25, 1.75),
        "bias_one": scatter_about(key_of[5], (C,), 0.5, 3.0, (), jnp.float32),
        "gain_two": jnp.clip(1.0 + 0.15 * jax.random.normal(key_of[6], (C,), jnp.float32), 0.25, 1.75),
        "bias_two": scatter_about(key_of[7], (C,), 0.5, 3.0, (), jnp.float32),
    }


epsilon = 1e-06

def normalize(field, gain, bias):
    groups = field.reshape(-1, GROUPS, C // GROUPS)
    centre = lax.optimization_barrier(jnp.mean(groups, axis=(0, 2), keepdims=True))
    spread = lax.optimization_barrier(jnp.mean((groups - centre) ** 2, axis=(0, 2), keepdims=True))
    centre_full = jnp.broadcast_to(centre[0], (GROUPS, C // GROUPS)).reshape(C)
    inv_std = jnp.broadcast_to(1.0 / jnp.sqrt(spread[0] + epsilon), (GROUPS, C // GROUPS)).reshape(C)
    unit = (field - centre_full) * inv_std
    inner = unit * gain + bias
    return (jax.nn.silu(inner).astype(jnp.bfloat16), unit, inner, inv_std)

def convolve(padded, weights):
    kernel = weights.reshape(3, 3, 3, C, C).astype(jnp.float32)
    result = lax.conv_general_dilated(padded.astype(jnp.float32)[None], kernel, (1, 1, 1), 'VALID', dimension_numbers=('NDHWC', 'DHWIO', 'NDHWC'), precision=lax.Precision.HIGHEST)
    return result[0]

def flipped(weights):
    whole = weights.reshape(3, 3, 3, C, C)
    return jnp.swapaxes(jnp.flip(whole, (0, 1, 2)), 3, 4).reshape(3, 9 * C, C)

def pad_past(field):
    return jnp.pad(field, ((2, 0), (1, 1), (1, 1), (0, 0)))

def pad_next(field):
    return jnp.pad(field, ((0, 2), (1, 1), (1, 1), (0, 0)))

def norm_back(grad_act, unit, inner, inv_std, gain):
    squash = jax.nn.sigmoid(inner)
    grad_inner = grad_act * squash * (1.0 + inner * (1.0 - squash))
    grad_gain = lax.optimization_barrier(jnp.sum(grad_inner * unit, axis=(0, 1, 2)))
    grad_bias = lax.optimization_barrier(jnp.sum(grad_inner, axis=(0, 1, 2)))
    members = NT * NH * NW * (C // GROUPS)
    first = jnp.repeat((gain * grad_bias).reshape(GROUPS, -1).sum(1), C // GROUPS) / members
    second = jnp.repeat((gain * grad_gain).reshape(GROUPS, -1).sum(1), C // GROUPS) / members
    grad_field = (grad_inner * gain - first - unit * second) * inv_std
    return (grad_field, grad_gain, grad_bias)

def reference(features, cotangent, conv_one, conv_two, gain_one, bias_one, gain_two, bias_two):
    act_one, unit_one, inner_one, inv_one = normalize(features, gain_one, bias_one)
    hidden = convolve(pad_past(act_one), conv_one)
    act_two, unit_two, inner_two, inv_two = normalize(hidden, gain_two, bias_two)
    branch = convolve(pad_past(act_two), conv_two)
    block_out = features + branch
    cotangent_low = cotangent.astype(jnp.bfloat16)
    grad_act_two = convolve(pad_next(cotangent_low), flipped(conv_two))
    grad_hidden, gain_grad_two, bias_grad_two = norm_back(grad_act_two, unit_two, inner_two, inv_two, gain_two)
    grad_act_one = convolve(pad_next(grad_hidden.astype(jnp.bfloat16)), flipped(conv_one))
    grad_field, gain_grad_one, bias_grad_one = norm_back(grad_act_one, unit_one, inner_one, inv_one, gain_one)
    grad_input = cotangent + grad_field
    norm_grads = jnp.stack([gain_grad_one, bias_grad_one, gain_grad_two, bias_grad_two])
    return (block_out, grad_input, norm_grads)
```

```python
import functools

import jax
import jax.numpy as jnp
from jax import lax
from jax.experimental import pallas as pl
from jax.experimental.pallas import tpu as pltpu
from jax.sharding import PartitionSpec as P

AXES = ("ta", "ha", "wa")
N = 8
C = 256
GROUP = 8
EPS = 1e-06
CELLS = 256
MESH = pl.DeviceIdType.MESH
F32 = jnp.float32
BF16 = jnp.bfloat16

FEAT, COT, HID, GRAD = range(4)
OWN = {FEAT: 2, COT: 0, HID: 2, GRAD: 0}
STEPS = {FEAT: (0, 1), COT: (0, -1), HID: (0, -1, 1), GRAD: (0, -1)}


def sigmoid(v):
    return 1.0 / (1.0 + jnp.exp(-v))


def group_sum(v):
    lane = lax.broadcasted_iota(jnp.int32, v.shape, 1)
    for s in (1, 2, 4):
        up = pltpu.roll(v, s, 1)
        down = pltpu.roll(v, C - s, 1)
        v = v + jnp.where((lane & s) != 0, up, down)
    return v


def kernel(
    feat, cot, w_one, w_two, gain_one, bias_one, gain_two, bias_two,
    block_out, grad_input, norm_grads,
    fx, cx, hx, gx, fk, ck, hk, gk, fq, cq, hq, gq, ks, qs,
    lhs_a, lhs_b, xs, xb, wb, stage, board, inner_grad, unit_buf, ga,
    local_sem, ar_s, ar_r, halo_s, halo_r, x_s, x_r, ring_s, ring_r, sib_s, sib_r,
):
    ta, ha, wa = (lax.axis_index(a) for a in AXES)
    me = (ta, ha, wa)
    core = lax.rem(wa, 2)
    sibling = (ta, ha, wa + 1 - 2 * core)
    fields = {FEAT: fx, COT: cx, HID: hx, GRAD: gx}
    cols = {FEAT: fk, COT: ck, HID: hk, GRAD: gk}
    corners = {FEAT: fq, COT: cq, HID: hq, GRAD: gq}

    def along(axis, k):
        spot = list(me)
        spot[axis] = lax.rem(me[axis] + k, N)
        return tuple(spot)

    barrier = pltpu.get_barrier_semaphore()
    count = 0
    for axis in range(3):
        for k in range(1, N):
            pl.semaphore_signal(barrier, inc=1, device_id=along(axis, k), device_id_type=MESH)
            count += 1
    for dt in (-1, 0, 1):
        for dh in (-1, 0, 1):
            for dw in (-1, 0, 1):
                if abs(dt) + abs(dh) + abs(dw) >= 2:
                    spot = tuple(lax.rem(m + d + N, N) for m, d in zip(me, (dt, dh, dw)))
                    pl.semaphore_signal(barrier, inc=1, device_id=spot, device_id_type=MESH)
                    count += 1

    load_f = pltpu.make_async_copy(feat, fx.at[pl.ds(2, 2), pl.ds(1, 8)], local_sem.at[0])
    load_c = pltpu.make_async_copy(cot, cx.at[pl.ds(0, 2), pl.ds(1, 8)], local_sem.at[1])
    load_f.start()
    load_c.start()

    def reduce_copies(k, s):
        axis = 2 - s
        return [
            pltpu.make_async_remote_copy(
                src_ref=stage.at[k, s],
                dst_ref=board.at[k, s, me[axis]],
                send_sem=ar_s.at[k, s],
                recv_sem=ar_r.at[k, s],
                device_id=along(axis, j),
                device_id_type=MESH,
            )
            for j in (4, 3, 5, 2, 6, 1, 7)
        ]

    def reduce_send(k, s, value):
        stage[k, s] = value
        board[k, s, me[2 - s]] = value
        for copy in reduce_copies(k, s):
            copy.start()

    def reduce_get(k, s):
        seven = board.at[k, s, pl.ds(0, N - 1)]
        pltpu.make_async_copy(seven, seven, ar_r.at[k, s]).wait()
        return board[k, s]

    def merge_moments(k, s):
        got = reduce_get(k, s)
        cells = float(CELLS * N**s)
        means, squares = got[:, 0:1, :], got[:, 1:2, :]
        mean = jnp.sum(means, axis=0) * (1.0 / N)
        off = means - mean[None]
        square = jnp.sum(squares, axis=0) + cells * jnp.sum(off * off, axis=0)
        return jnp.concatenate([mean, square], axis=0)

    def merge_sums(k, s):
        return jnp.sum(reduce_get(k, s), axis=0)

    def local_moments(ref, own):
        v = ref[pl.ds(own, 2), pl.ds(1, 8)].reshape(CELLS, C)
        mean = jnp.sum(v, axis=0, keepdims=True) * (1.0 / CELLS)
        d = v - mean
        return jnp.concatenate([mean, jnp.sum(d * d, axis=0, keepdims=True)], axis=0)

    def finish_moments(pair):
        cells = float(CELLS * N**3)
        mean, square = pair[0:1], pair[1:2]
        centre = group_sum(mean) * (1.0 / GROUP)
        off = mean - centre
        spread = group_sum(square + cells * off * off) * (1.0 / (cells * GROUP))
        return centre, 1.0 / jnp.sqrt(spread + EPS)

    def halo_messages(field):
        own, x, k, q = OWN[field], fields[field], cols[field], corners[field]
        src_t = pl.ds(own, 2)
        for dt in STEPS[field]:
            dst_t = pl.ds(own - 2 * dt, 2)
            for dh in (0, -1, 1):
                for dw in (0, -1, 1):
                    if (dt, dh, dw) == (0, 0, 0):
                        continue
                    r, b = int(dw > 0), int(dh > 0)
                    if dh == 0 and dw == 0:
                        src, dst = x.at[src_t, pl.ds(1, 8)], x.at[dst_t, pl.ds(1, 8)]
                    elif dw == 0:
                        src, dst = x.at[src_t, 8 if b else 1], x.at[dst_t, 0 if b else 9]
                    elif dh == 0:
                        src, dst = ks.at[field, r], k.at[1 - r, dst_t]
                    else:
                        src, dst = qs.at[field, r, b], q.at[1 - r, 1 - b, dst_t]
                    spot = (ta + dt, ha + dh, wa + dw)
                    back = (ta - dt, ha - dh, wa - dw)
                    number = (dt + 1) * 9 + (dh + 1) * 3 + dw + 1
                    copy = pltpu.make_async_remote_copy(
                        src_ref=src, dst_ref=dst,
                        send_sem=halo_s.at[field, number], recv_sem=halo_r.at[field, number],
                        device_id=spot, device_id_type=MESH,
                    )
                    yield copy, inside(spot, (dt, dh, dw)), inside(back, (-dt, -dh, -dw))

    def inside(spot, delta):
        ok = None
        for v, d in zip(spot, delta):
            if d:
                one = v < N if d > 0 else v >= 0
                ok = one if ok is None else jnp.logical_and(ok, one)
        return ok

    def halo_send(field):
        own, x = OWN[field], fields[field]
        for r, w in ((0, 0), (1, 15)):
            for t in range(2):
                for h in range(8):
                    row = x[own + t, 1 + h, w : w + 1, :]
                    ks[field, r, t, h : h + 1, :] = row
                    if h in (0, 7):
                        qs[field, r, h // 7, t] = row
        for copy, goes, _ in halo_messages(field):
            pl.when(goes)(copy.start)

    def halo_wait(field):
        for copy, _, comes in halo_messages(field):
            pl.when(comes)(copy.wait_recv)

    def halo_done(field):
        for copy, goes, _ in halo_messages(field):
            pl.when(goes)(copy.wait_send)

    shift = 4 * lax.rem(wa, 4)

    def shard_stage(conv, ref):
        for a in range(3):
            rows = jnp.concatenate([ref[a].astype(F32), jnp.zeros((12, C), F32)], axis=0)
            rows = pltpu.roll(rows, shift, 0).astype(BF16)
            xs[conv, a] = rows
            xb[conv, wa, a] = rows

    def shard_copies(conv):
        return [
            pltpu.make_async_remote_copy(
                src_ref=xs.at[conv], dst_ref=xb.at[conv, wa],
                send_sem=x_s.at[conv], recv_sem=x_r.at[conv],
                device_id=along(2, j), device_id_type=MESH,
            )
            for j in range(1, N)
        ]

    def shard_send(conv):
        for copy in shard_copies(conv):
            copy.start()

    def shard_merge(conv):
        seven = xb.at[conv, pl.ds(0, N - 1)]
        pltpu.make_async_copy(seven, seven, x_r.at[conv]).wait()
        for a in range(3):
            for g in range(2):
                parts = [[xb[conv, 4 * g + p, a, 16 * i : 16 * i + 16, :] for i in range(3)] for p in range(4)]
                tiles = [parts[0][0], parts[0][1]]
                for p in range(1, 4):
                    tiles.append(parts[p - 1][2] + parts[p][0])
                    tiles.append(parts[p][1])
                tiles.append(parts[3][2])
                for i, tile in enumerate(tiles):
                    wb[conv, a, 18 * ha + 9 * g + i] = tile

    def piece(conv, way, step, half):
        block = lax.rem(ha - step + N, N) if way == 0 else lax.rem(ha + step, N)
        taps = pl.ds(0, 3) if step < 4 else (pl.ds(0, 2) if way == 0 else pl.ds(2, 1))
        return wb.at[conv, taps, pl.ds(18 * block + 9 * half, 9)]

    def ring_copy(conv, way, step):
        block = lax.rem(ha - (step - 1) + N, N) if way == 0 else lax.rem(ha + step - 1, N)
        taps = pl.ds(0, 3) if step < 4 else (pl.ds(0, 2) if way == 0 else pl.ds(2, 1))
        ref = wb.at[conv, taps, pl.ds(18 * block + 9 * core, 9)]
        return pltpu.make_async_remote_copy(
            src_ref=ref, dst_ref=ref,
            send_sem=ring_s.at[conv, way, step - 1], recv_sem=ring_r.at[conv, way, step - 1],
            device_id=along(1, 1 if way == 0 else N - 1), device_id_type=MESH,
        )

    def sibling_copy(conv, way, step):
        ref = piece(conv, way, step, core)
        return pltpu.make_async_remote_copy(
            src_ref=ref, dst_ref=ref,
            send_sem=sib_s.at[conv, way, step - 1], recv_sem=sib_r.at[conv, way, step - 1],
            device_id=sibling, device_id_type=MESH,
        )

    def ring_start(conv):
        for way in (0, 1):
            ring_copy(conv, way, 1).start()

    def ring_step(conv, step):
        for way in (0, 1):
            got = piece(conv, way, step, core)
            pltpu.make_async_copy(got, got, ring_r.at[conv, way, step - 1]).wait()
            if step < 4:
                ring_copy(conv, way, step + 1).start()
            sibling_copy(conv, way, step).start()

    def sibling_wait(conv):
        for step in range(1, 5):
            for way in (0, 1):
                got = piece(conv, way, step, 1 - core)
                pltpu.make_async_copy(got, got, sib_r.at[conv, way, step - 1]).wait()

    def weights_done(conv):
        for copy in shard_copies(conv):
            copy.wait_send()
        for step in range(1, 5):
            for way in (0, 1):
                ring_copy(conv, way, step).wait_send()
                sibling_copy(conv, way, step).wait_send()

    row_of = lax.broadcasted_iota(jnp.int32, (16, C), 0)

    def fill(lhs, refs, first, early, late, fn, flip):
        groups = [tuple(r[0] for r in refs), tuple(r[1] for r in refs), tuple(r[2] for r in refs)]
        xs_, ks_, qs_ = groups
        top, bottom, left, right = ha > 0, ha < N - 1, wa > 0, wa < N - 1

        def body(t, carry):
            src = t + first
            frame = jnp.logical_and(jnp.logical_or(t >= 2, early), jnp.logical_or(t < 2, late))
            sides = []
            for r, ok in ((0, left), (1, right)):
                ok = jnp.logical_and(ok, frame)
                mid = jnp.where(ok, fn(*[k[r, src] for k in ks_]), 0.0)
                hi = jnp.where(jnp.logical_and(ok, top), fn(*[q[r, 0, src] for q in qs_]), 0.0)
                lo = jnp.where(jnp.logical_and(ok, bottom), fn(*[q[r, 1, src] for q in qs_]), 0.0)
                sides.append([hi] + [mid[h : h + 1] for h in range(8)] + [lo])
            for h in range(10):
                ok = frame
                if h == 0:
                    ok = jnp.logical_and(ok, top)
                if h == 9:
                    ok = jnp.logical_and(ok, bottom)
                v = jnp.where(ok, fn(*[x[src, h] for x in xs_]), 0.0)
                before = jnp.where(row_of == 0, sides[0][h], pltpu.roll(v, 1, 0))
                after = jnp.where(row_of == 15, sides[1][h], pltpu.roll(v, 15, 0))
                if flip:
                    before, after = after, before
                lhs[t, h, :, 0:C] = before.astype(BF16)
                lhs[t, h, :, C : 2 * C] = v.astype(BF16)
                lhs[t, h, :, 2 * C : 3 * C] = after.astype(BF16)
            return carry

        lax.fori_loop(0, 4, body, 0)

    def convolve(lhs, conv, flip):
        total = None
        for a in range(3):
            for b in range(3):
                part = lhs[a : a + 2, b : b + 8].reshape(CELLS, 3 * C)
                if flip:
                    w = wb[conv, 2 - a, pl.ds(48 * (2 - b), 48)].reshape(3 * C, C)
                    out = None
                    for c in range(3):
                        one = lax.dot_general(
                            part[:, c * C : c * C + C], w[c * C : c * C + C, :],
                            (((1,), (1,)), ((), ())), preferred_element_type=F32,
                        )
                        out = one if out is None else out + one
                else:
                    w = wb[conv, a, pl.ds(48 * b, 48)].reshape(3 * C, C)
                    out = jnp.dot(part, w, preferred_element_type=F32)
                total = out if total is None else total + out
        return total.reshape(2, 8, 16, C)

    shard_stage(0, w_one)
    shard_stage(1, w_two)
    load_f.wait()
    moments = local_moments(fx, 2)
    pl.semaphore_wait(barrier, count)
    reduce_send(0, 0, moments)
    shard_send(0)
    halo_send(FEAT)
    shard_send(1)
    load_c.wait()
    halo_send(COT)
    reduce_send(0, 1, merge_moments(0, 0))
    shard_merge(0)
    ring_start(0)
    reduce_send(0, 2, merge_moments(0, 1))
    shard_merge(1)
    ring_step(0, 1)
    ring_start(1)
    centre_1, inv_1 = finish_moments(merge_moments(0, 2))
    g1, b1, g2, b2 = gain_one[...], bias_one[...], gain_two[...], bias_two[...]
    halo_wait(FEAT)

    def act_one(v):
        inner = (v - centre_1) * inv_1 * g1 + b1
        return inner * sigmoid(inner)

    fill(lhs_a, [(fx, fk, fq)], 0, ta > 0, True, act_one, False)
    ring_step(0, 2)
    halo_wait(COT)
    fill(lhs_b, [(cx, ck, cq)], 0, True, ta < N - 1, lambda v: v, True)
    ring_step(0, 3)
    ring_step(0, 4)
    sibling_wait(0)

    hx[pl.ds(2, 2), pl.ds(1, 8)] = convolve(lhs_a, 0, False)
    reduce_send(1, 0, local_moments(hx, 2))
    halo_send(HID)
    ring_step(1, 1)
    reduce_send(1, 1, merge_moments(1, 0))
    ring_step(1, 2)
    reduce_send(1, 2, merge_moments(1, 1))
    ring_step(1, 3)
    ring_step(1, 4)
    sibling_wait(1)
    gx[pl.ds(0, 2), pl.ds(1, 8)] = convolve(lhs_b, 1, True)
    halo_send(GRAD)
    centre_2, inv_2 = finish_moments(merge_moments(1, 2))

    def back_sums(field, own, grad, centre, inv, gain, bias):
        def body(i, carry):
            gain_sum, bias_sum = carry
            t, h = i // 8, i % 8
            unit = (field[own + t, 1 + h] - centre) * inv
            inner = unit * gain + bias
            s = sigmoid(inner)
            gi = grad(t, h) * s * (1.0 + inner * (1.0 - s))
            inner_grad[i] = gi
            unit_buf[i] = unit
            return gain_sum + gi * unit, bias_sum + gi

        zero = jnp.zeros((16, C), F32)
        sums = lax.fori_loop(0, 16, body, (zero, zero))
        return jnp.concatenate([jnp.sum(s, axis=0, keepdims=True) for s in sums], axis=0)

    reduce_send(2, 0, back_sums(hx, 2, lambda t, h: gx[t, 1 + h], centre_2, inv_2, g2, b2))
    halo_wait(HID)

    def act_two(v):
        inner = (v - centre_2) * inv_2 * g2 + b2
        return inner * sigmoid(inner)

    fill(lhs_a, [(hx, hk, hq)], 0, ta > 0, True, act_two, False)
    reduce_send(2, 1, merge_sums(2, 0))
    block_out[...] = fx[pl.ds(2, 2), pl.ds(1, 8)] + convolve(lhs_a, 1, False)
    reduce_send(2, 2, merge_sums(2, 1))
    halo_wait(GRAD)
    sums_2 = merge_sums(2, 2)
    norm_grads[2:4, :] = sums_2
    members = float(CELLS * N**3 * GROUP)
    both = group_sum(sums_2 * g2) * (1.0 / members)
    first_2, second_2 = both[1:2], both[0:1]

    def grad_hidden(v, g):
        unit = (v - centre_2) * inv_2
        inner = unit * g2 + b2
        s = sigmoid(inner)
        gi = g * s * (1.0 + inner * (1.0 - s))
        return (gi * g2 - first_2 - unit * second_2) * inv_2

    class Shifted:
        def __init__(self, ref, lead):
            self.ref, self.lead = ref, lead

        def __getitem__(self, idx):
            idx = idx if isinstance(idx, tuple) else (idx,)
            n = self.lead
            return self.ref[idx[:n] + (idx[n] + 2,) + idx[n + 1 :]]

    fill(
        lhs_b,
        [(Shifted(hx, 0), Shifted(hk, 1), Shifted(hq, 2)), (gx, gk, gq)],
        0, True, ta < N - 1, grad_hidden, True,
    )
    grad_act = convolve(lhs_b, 0, True)
    ga[...] = grad_act

    reduce_send(3, 0, back_sums(fx, 2, lambda t, h: ga[t, h], centre_1, inv_1, g1, b1))
    for field in (FEAT, COT, HID):
        halo_done(field)
    reduce_send(3, 1, merge_sums(3, 0))
    for conv in (0, 1):
        weights_done(conv)
    reduce_send(3, 2, merge_sums(3, 1))
    halo_done(GRAD)
    sums_1 = merge_sums(3, 2)
    norm_grads[0:2, :] = sums_1
    both = group_sum(sums_1 * g1) * (1.0 / members)
    first_1, second_1 = both[1:2], both[0:1]

    def last(i, carry):
        t, h = i // 8, i % 8
        field = (inner_grad[i] * g1 - first_1 - unit_buf[i] * second_1) * inv_1
        grad_input[t, h] = cx[t, 1 + h] + field
        return carry

    lax.fori_loop(0, 16, last, 0)
    for k in range(4):
        for s in range(3):
            for copy in reduce_copies(k, s):
                copy.wait_send()


def shards(features, cotangent, conv_one, conv_two, gain_one, bias_one, gain_two, bias_two):
    vmem = pl.BlockSpec(memory_space=pltpu.VMEM)
    anywhere = pl.BlockSpec(memory_space=pl.ANY)

    def buf(*shape, dtype=F32):
        return pltpu.VMEM(shape, dtype)

    scratch = (
        [buf(t, 10, 16, C) for t in (4, 4, 6, 4)]
        + [buf(2, t, 8, C) for t in (4, 4, 6, 4)]
        + [buf(2, 2, t, 1, C) for t in (4, 4, 6, 4)]
        + [buf(4, 2, 2, 8, C), buf(4, 2, 2, 2, 1, C)]
        + [buf(4, 10, 16, 3 * C, dtype=BF16)] * 2
        + [buf(2, 3, 48, C, dtype=BF16), buf(2, N, 3, 48, C, dtype=BF16)]
        + [buf(2, 3, 144, 16, C, dtype=BF16)]
        + [buf(4, 3, 2, C), buf(4, 3, N, 2, C)]
        + [buf(16, 16, C)] * 2
        + [buf(2, 8, 16, C)]
        + [pltpu.SemaphoreType.DMA((2,))]
        + [pltpu.SemaphoreType.DMA((4, 3))] * 2
        + [pltpu.SemaphoreType.DMA((4, 27))] * 2
        + [pltpu.SemaphoreType.DMA((2,))] * 2
        + [pltpu.SemaphoreType.DMA((2, 2, 4))] * 4
    )
    block = jax.ShapeDtypeStruct((2, 8, 16, C), F32)
    return pl.pallas_call(
        kernel,
        out_shape=(block, block, jax.ShapeDtypeStruct((4, C), F32)),
        in_specs=[anywhere] * 2 + [vmem] * 6,
        out_specs=(vmem, vmem, vmem),
        scratch_shapes=scratch,
        compiler_params=pltpu.CompilerParams(
            collective_id=0, has_side_effects=True, vmem_limit_bytes=56 * 2**20
        ),
    )(
        features, cotangent, conv_one, conv_two,
        gain_one[None], bias_one[None], gain_two[None], bias_two[None],
    )


def solution(mesh):
    return jax.shard_map(
        shards,
        mesh=mesh,
        in_specs=(
            P("ta", "ha", "wa", None),
            P("ta", "ha", "wa", None),
            P(None, ("ha", "wa"), None),
            P(None, ("ha", "wa"), None),
            P(),
            P(),
            P(),
            P(),
        ),
        out_specs=(P("ta", "ha", "wa", None), P("ta", "ha", "wa", None), P()),
        check_vma=False,
    )
```

```python
import functools

import jax
import jax.numpy as jnp
from jax import lax
from jax.experimental import pallas as pl
from jax.experimental.pallas import tpu as pltpu
from jax.sharding import PartitionSpec as P

AXES = ("ta", "ha", "wa")
N = 8
C = 256
GROUP = 8
NEAR = (1, 7, 2, 6, 3, 5, 4)
EPS = 1e-06
CELLS = 256
MESH = pl.DeviceIdType.MESH
F32 = jnp.float32
BF16 = jnp.bfloat16

FEAT, HID, GRAD, COT, ACT = range(5)
NARROW = (COT, ACT)
OWN = {FEAT: 2, HID: 0, GRAD: 0, COT: 0, ACT: 2}


def sigmoid(v):
    return 1.0 / (1.0 + jnp.exp(-v))


def group_sum(v):
    lane = lax.broadcasted_iota(jnp.int32, v.shape, 1)
    for s in (1, 2, 4):
        up = pltpu.roll(v, s, 1)
        down = pltpu.roll(v, C - s, 1)
        v = v + jnp.where((lane & s) != 0, up, down)
    return v


def kernel(
    feat, cot, w_one, w_two, gain_one, bias_one, gain_two, bias_two,
    block_out, grad_input, norm_grads,
    cx, fx, hx, gx, nx, mx, fk, hk, gk, nk, mk, fq, hq, gq, nq, mq, ks, qs, ns, ms,
    lhs_a, lhs_b, shards_in, wb, stage, board, inner_grad, unit_buf, ga,
    local_sem, ar_s, ar_r, halo_s, halo_r, y_s, y_r, x_s, x_r, z_s, z_r, c_s, c_r,
):
    ta, ha, wa = (lax.axis_index(a) for a in AXES)
    me = (ta, ha, wa)
    core = lax.rem(wa, 2)
    sibling = (ta, ha, wa + 1 - 2 * core)
    fields = {FEAT: fx, HID: hx, GRAD: gx, COT: nx, ACT: mx}
    cols = {FEAT: fk, HID: hk, GRAD: gk, COT: nk, ACT: mk}
    corners = {FEAT: fq, HID: hq, GRAD: gq, COT: nq, ACT: mq}

    def along(axis, k):
        spot = list(me)
        spot[axis] = lax.rem(me[axis] + k, N)
        return tuple(spot)

    barrier = pltpu.get_barrier_semaphore()
    count = 0
    for axis in range(3):
        for k in range(1, N):
            pl.semaphore_signal(barrier, inc=1, device_id=along(axis, k), device_id_type=MESH)
            count += 1
    for dt in (-1, 0, 1):
        for dh in (-1, 0, 1):
            for dw in (-1, 0, 1):
                if abs(dt) + abs(dh) + abs(dw) >= 2:
                    spot = tuple(lax.rem(m + d + N, N) for m, d in zip(me, (dt, dh, dw)))
                    pl.semaphore_signal(barrier, inc=1, device_id=spot, device_id_type=MESH)
                    count += 1

    load_f = pltpu.make_async_copy(feat, fx.at[pl.ds(2, 2), pl.ds(1, 8)], local_sem.at[0])
    load_c = pltpu.make_async_copy(cot, cx, local_sem.at[1])
    load_f.start()
    load_c.start()

    def reduce_copies(k, s):
        axis = 2 - s
        return [
            pltpu.make_async_remote_copy(
                src_ref=stage.at[k, s],
                dst_ref=board.at[k, s, me[axis]],
                send_sem=ar_s.at[k, s],
                recv_sem=ar_r.at[k, s],
                device_id=along(axis, j),
                device_id_type=MESH,
            )
            for j in (4, 3, 5, 2, 6, 1, 7)
        ]

    def reduce_send(k, s, value):
        stage[k, s] = value
        board[k, s, me[2 - s]] = value
        for copy in reduce_copies(k, s):
            copy.start()

    def reduce_get(k, s):
        seven = board.at[k, s, pl.ds(0, N - 1)]
        pltpu.make_async_copy(seven, seven, ar_r.at[k, s]).wait()
        return board[k, s]

    def merge_moments(k, s):
        got = reduce_get(k, s)
        cells = float(CELLS * N**s)
        means, squares = got[:, 0:1, :], got[:, 1:2, :]
        mean = jnp.sum(means, axis=0) * (1.0 / N)
        off = means - mean[None]
        square = jnp.sum(squares, axis=0) + cells * jnp.sum(off * off, axis=0)
        return jnp.concatenate([mean, square], axis=0)

    def merge_sums(k, s):
        return jnp.sum(reduce_get(k, s), axis=0)

    def local_moments(ref, own):
        v = ref[pl.ds(own, 2), pl.ds(1, 8)].reshape(CELLS, C)
        mean = jnp.sum(v, axis=0, keepdims=True) * (1.0 / CELLS)
        d = v - mean
        return jnp.concatenate([mean, jnp.sum(d * d, axis=0, keepdims=True)], axis=0)

    def finish_moments(pair):
        cells = float(CELLS * N**3)
        mean, square = pair[0:1], pair[1:2]
        centre = group_sum(mean) * (1.0 / GROUP)
        off = mean - centre
        spread = group_sum(square + cells * off * off) * (1.0 / (cells * GROUP))
        return centre, 1.0 / jnp.sqrt(spread + EPS)

    def halo_messages(field):
        own, x, k, q = OWN[field], fields[field], cols[field], corners[field]
        src_t = pl.ds(own, 2)
        narrow = field in NARROW
        for dt in (0, 1 if own else -1):
            dst_t = pl.ds(own - 2 * dt, 2)
            dst_k = (own - 2 * dt) // 2 if narrow else dst_t
            for dh in (0, -1, 1):
                for dw in (0, -1, 1):
                    if (dt, dh, dw) == (0, 0, 0):
                        continue
                    r, b = int(dw > 0), int(dh > 0)
                    if dh == 0 and dw == 0:
                        src, dst = x.at[src_t, pl.ds(1, 8)], x.at[dst_t, pl.ds(1, 8)]
                    elif dw == 0:
                        src, dst = x.at[src_t, 8 if b else 1], x.at[dst_t, 0 if b else 9]
                    elif dh == 0:
                        src = ns.at[field - COT, r] if narrow else ks.at[field, r]
                        dst = k.at[1 - r, dst_k]
                    else:
                        src = ms.at[field - COT, r, b] if narrow else qs.at[field, r, b]
                        dst = q.at[1 - r, 1 - b, dst_k]
                    spot = (ta + dt, ha + dh, wa + dw)
                    back = (ta - dt, ha - dh, wa - dw)
                    number = (dt + 1) * 9 + (dh + 1) * 3 + dw + 1
                    copy = pltpu.make_async_remote_copy(
                        src_ref=src, dst_ref=dst,
                        send_sem=halo_s.at[field, number], recv_sem=halo_r.at[field, number],
                        device_id=spot, device_id_type=MESH,
                    )
                    yield copy, inside(spot, (dt, dh, dw)), inside(back, (-dt, -dh, -dw))

    def inside(spot, delta):
        ok = None
        for v, d in zip(spot, delta):
            if d:
                one = v < N if d > 0 else v >= 0
                ok = one if ok is None else jnp.logical_and(ok, one)
        return ok

    def halo_send(field):
        own, x = OWN[field], fields[field]
        for r, w in ((0, 0), (1, 15)):
            if field in NARROW:
                ns[field - COT, r] = x[own : own + 2, 1:9, w, :].astype(F32).reshape(16, C).astype(BF16)
                for b, h in ((0, 1), (1, 8)):
                    pair = [x[own + t, h, w : w + 1, :].astype(F32) for t in range(2)]
                    ms[field - COT, r, b] = jnp.concatenate(pair + [jnp.zeros((14, C), F32)], axis=0).astype(BF16)
                continue
            for t in range(2):
                for h in range(8):
                    row = x[own + t, 1 + h, w : w + 1, :]
                    ks[field, r, t, h : h + 1, :] = row
                    if h in (0, 7):
                        qs[field, r, h // 7, t] = row
        for copy, goes, _ in halo_messages(field):
            pl.when(goes)(copy.start)

    def halo_wait(field):
        for copy, _, comes in halo_messages(field):
            pl.when(comes)(copy.wait_recv)

    def halo_done(field):
        for copy, goes, _ in halo_messages(field):
            pl.when(goes)(copy.wait_send)

    shift = 4 * lax.rem(wa, 4)
    half = lax.rem(ta, 2)
    column = lax.div(wa, 2)

    def block(j):
        return lax.rem(ha - j + N, N)

    row_half = lax.broadcasted_iota(jnp.int32, (16, C // 2), 0)

    def shard_stage(conv, ref):
        spare = None
        for a in range(3):
            rows = jnp.concatenate([ref[a].astype(F32), jnp.zeros((12, C), F32)], axis=0)
            rows = pltpu.roll(rows, shift, 0)
            rows = jnp.where(half == 0, rows[:, : C // 2], rows[:, C // 2 :])
            first, middle, end = rows[0:16], rows[16:32], rows[32:48]
            shards_in[conv, ha, core, half, column, 2 * a] = jnp.where(row_half >= shift, first, end).astype(BF16)
            shards_in[conv, ha, core, half, column, 2 * a + 1] = middle.astype(BF16)
            end = pltpu.roll(end, lax.rem(4 * a - shift + 16, 16), 0)
            spare = end if a == 0 else jnp.where(row_half >= 4 * a, end, spare)
        shards_in[conv, ha, core, half, column, 6] = spare.astype(BF16)

    def weight_copy(ref, sems, spot, device):
        return pltpu.make_async_remote_copy(
            src_ref=ref, dst_ref=ref, send_sem=sems[0].at[spot], recv_sem=sems[1].at[spot],
            device_id=device, device_id_type=MESH,
        )

    def along_ha(conv):
        ref = shards_in.at[conv, ha, core, half, column]
        return [weight_copy(ref, (y_s, y_r), (conv, j), along(1, j)) for j in NEAR]

    def along_wa(conv, j):
        ref = shards_in.at[conv, block(j), core, half, column]
        return [weight_copy(ref, (x_s, x_r), (conv, j), along(2, k)) for k in (2, 6, 4)]

    def along_ta(conv, j):
        ref = shards_in.at[conv, block(j), core, half]
        return [
            weight_copy(ref.at[pl.ds(0, 2)], (z_s, z_r), (conv, j, 0), along(0, 1)),
            weight_copy(ref.at[pl.ds(2, 2)], (z_s, z_r), (conv, j, 1), along(0, N - 1)),
        ]

    def across(conv, j):
        return [weight_copy(shards_in.at[conv, block(j), core], (c_s, c_r), (conv, j), sibling)]

    def start(copies):
        for copy in copies:
            copy.start()

    def arrived(ref, sem):
        pltpu.make_async_copy(ref, ref, sem).wait()

    def weights_out(conv):
        start(along_ha(conv))
        start(along_wa(conv, 0))

    def from_ha(conv, j):
        arrived(shards_in.at[conv, block(j), core, half, 0], y_r.at[conv, j])
        start(along_wa(conv, j))

    def from_wa(conv, j):
        arrived(shards_in.at[conv, block(j), core, half, pl.ds(0, 3)], x_r.at[conv, j])
        start(along_ta(conv, j))

    def from_ta(conv, j):
        ref = shards_in.at[conv, block(j), core, 1 - half]
        arrived(ref.at[pl.ds(0, 2)], z_r.at[conv, j, 0])
        arrived(ref.at[pl.ds(2, 2)], z_r.at[conv, j, 1])
        start(across(conv, j))

    def from_sibling(conv, j):
        arrived(shards_in.at[conv, block(j), 1 - core], c_r.at[conv, j])
        spot = block(j)

        def merge(g, carry):
            for s in range(2):
                def tile(p, i):
                    return shards_in[conv, spot, p % 2, s, 2 * g + p // 2, i].astype(F32)

                spare = [tile(p, 6) for p in range(4)]
                for a in range(3):
                    heads = [tile(p, 2 * a) for p in range(4)]
                    tiles = [heads[0]]
                    for p in range(4):
                        tiles.append(tile(p, 2 * a + 1))
                        end = pltpu.roll(spare[p], (4 * (p - a)) % 16, 0) if p != a else spare[p]
                        if p < 3:
                            end = jnp.where(row_half < 4 * p + 4, end, heads[p + 1])
                        tiles.append(jnp.where(row_half < 4 * p, heads[p], end) if p else end)
                    for i, value in enumerate(tiles):
                        wb[conv, a, 18 * spot + 9 * g + i, :, s * (C // 2) : (s + 1) * (C // 2)] = value.astype(BF16)
            return carry

        lax.fori_loop(0, 2, merge, 0)

    def weights_done(conv):
        copies = along_ha(conv)
        for j in range(N):
            copies += along_wa(conv, j) + along_ta(conv, j) + across(conv, j)
        for copy in copies:
            copy.wait_send()

    row_of = lax.broadcasted_iota(jnp.int32, (16, C), 0)

    top, bottom, left, right = ha > 0, ha < N - 1, wa > 0, wa < N - 1

    def put(lhs, t, h, v, before, after, flip):
        before = jnp.where(row_of == 0, before, pltpu.roll(v, 1, 0))
        after = jnp.where(row_of == 15, after, pltpu.roll(v, 15, 0))
        if flip:
            before, after = after, before
        lhs[t, h, :, 0:C] = before.astype(BF16)
        lhs[t, h, :, C : 2 * C] = v.astype(BF16)
        lhs[t, h, :, 2 * C : 3 * C] = after.astype(BF16)

    def fill_frame(lhs, t, frame, cell, side, corner, flip):
        edges = []
        for r, ok in ((0, left), (1, right)):
            ok = jnp.logical_and(ok, frame)
            mid = jnp.where(ok, side(r), 0.0)
            hi = jnp.where(jnp.logical_and(ok, top), corner(r, 0), 0.0)
            lo = jnp.where(jnp.logical_and(ok, bottom), corner(r, 1), 0.0)
            edges.append([hi] + [mid[h : h + 1] for h in range(8)] + [lo])
        for h in range(10):
            ok = frame
            if h == 0:
                ok = jnp.logical_and(ok, top)
            if h == 9:
                ok = jnp.logical_and(ok, bottom)
            put(lhs, t, h, jnp.where(ok, cell(h), 0.0), edges[0][h], edges[1][h], flip)

    def fill(lhs, refs, early, late, fn, flip):
        def body(t, carry):
            frame = jnp.logical_and(jnp.logical_or(t >= 2, early), jnp.logical_or(t < 2, late))
            fill_frame(
                lhs, t, frame,
                lambda h: fn(*[x[t, h] for x, _, _ in refs]),
                lambda r: fn(*[k[r, t] for _, k, _ in refs]),
                lambda r, b: fn(*[q[r, b, t] for _, _, q in refs]),
                flip,
            )
            return carry

        lax.fori_loop(0, 4, body, 0)

    def fill_narrow(lhs, field, flip):
        x, k, q, own = fields[field], cols[field], corners[field], OWN[field] // 2
        for t in range(4):
            w, u = t // 2, t % 2
            frame = True if w == own else (ta > 0 if own else ta < N - 1)
            fill_frame(
                lhs, t, frame,
                lambda h: x[t, h].astype(F32),
                lambda r: k[r, w].astype(F32)[8 * u : 8 * u + 8],
                lambda r, b: q[r, b, w].astype(F32)[u : u + 1],
                flip,
            )

    def convolve(lhs, conv, flip):
        total = None
        for a in range(3):
            for b in range(3):
                part = lhs[a : a + 2, b : b + 8].reshape(CELLS, 3 * C)
                if flip:
                    w = wb[conv, 2 - a, pl.ds(48 * (2 - b), 48)].reshape(3 * C, C)
                    out = None
                    for c in range(3):
                        one = lax.dot_general(
                            part[:, c * C : c * C + C], w[c * C : c * C + C, :],
                            (((1,), (1,)), ((), ())), preferred_element_type=F32,
                        )
                        out = one if out is None else out + one
                else:
                    w = wb[conv, a, pl.ds(48 * b, 48)].reshape(3 * C, C)
                    out = jnp.dot(part, w, preferred_element_type=F32)
                total = out if total is None else total + out
        return total.reshape(2, 8, 16, C)

    shard_stage(0, w_one)
    shard_stage(1, w_two)
    load_f.wait()
    moments = local_moments(fx, 2)
    pl.semaphore_wait(barrier, count)
    reduce_send(0, 0, moments)
    weights_out(0)
    halo_send(FEAT)
    reduce_send(0, 1, merge_moments(0, 0))
    from_ha(0, 1)
    from_ha(0, 7)
    from_wa(0, 0)
    from_ha(0, 2)
    from_ha(0, 6)
    from_wa(0, 1)
    reduce_send(0, 2, merge_moments(0, 1))
    from_ha(0, 3)
    from_ha(0, 5)
    from_ha(0, 4)
    from_wa(0, 7)
    from_ta(0, 0)
    from_wa(0, 2)
    weights_out(1)
    from_ta(0, 1)
    centre_1, inv_1 = finish_moments(merge_moments(0, 2))
    g1, b1, g2, b2 = gain_one[...], bias_one[...], gain_two[...], bias_two[...]
    halo_wait(FEAT)

    def act_one(v):
        inner = (v - centre_1) * inv_1 * g1 + b1
        return inner * sigmoid(inner)

    fill(lhs_a, [(fx, fk, fq)], ta > 0, True, act_one, False)
    from_wa(0, 6)
    from_ta(0, 7)
    from_sibling(0, 0)
    from_wa(0, 3)
    from_ta(0, 2)
    from_sibling(0, 1)
    from_wa(0, 5)
    from_ta(0, 6)
    from_sibling(0, 7)
    from_wa(0, 4)
    load_c.wait()
    nx[pl.ds(0, 2), pl.ds(1, 8)] = cx[...].astype(BF16)
    halo_send(COT)
    for j in NEAR:
        from_ha(1, j)
    from_ta(0, 3)
    from_sibling(0, 2)
    from_ta(0, 5)
    from_sibling(0, 6)
    from_ta(0, 4)
    from_sibling(0, 3)
    from_sibling(0, 5)
    from_sibling(0, 4)

    hx[pl.ds(0, 2), pl.ds(1, 8)] = convolve(lhs_a, 0, False)
    reduce_send(1, 0, local_moments(hx, 0))
    for j in (0, 1, 7):
        from_wa(1, j)
    reduce_send(1, 1, merge_moments(1, 0))
    for j, k in ((2, 0), (6, 1), (3, 7)):
        from_wa(1, j)
        from_ta(1, k)
    reduce_send(1, 2, merge_moments(1, 1))
    for j, k, m in ((5, 2, 0), (4, 6, 1)):
        from_wa(1, j)
        from_ta(1, k)
        from_sibling(1, m)
    halo_send(HID)
    for j, k in ((3, 7), (5, 2), (4, 6)):
        from_ta(1, j)
        from_sibling(1, k)
    for j in (3, 5, 4):
        from_sibling(1, j)
    halo_wait(COT)
    fill_narrow(lhs_b, COT, True)
    gx[pl.ds(0, 2), pl.ds(1, 8)] = convolve(lhs_b, 1, True)
    halo_send(GRAD)
    centre_2, inv_2 = finish_moments(merge_moments(1, 2))

    def back_sums(field, own, grad, centre, inv, gain, bias):
        def body(i, carry):
            gain_sum, bias_sum = carry
            t, h = i // 8, i % 8
            unit = (field[own + t, 1 + h] - centre) * inv
            inner = unit * gain + bias
            s = sigmoid(inner)
            gi = grad(t, h) * s * (1.0 + inner * (1.0 - s))
            inner_grad[i] = gi
            unit_buf[i] = unit
            return gain_sum + gi * unit, bias_sum + gi

        zero = jnp.zeros((16, C), F32)
        sums = lax.fori_loop(0, 16, body, (zero, zero))
        return jnp.concatenate([jnp.sum(s, axis=0, keepdims=True) for s in sums], axis=0)

    reduce_send(2, 0, back_sums(hx, 0, lambda t, h: gx[t, 1 + h], centre_2, inv_2, g2, b2))

    def act_two(i, carry):
        inner = unit_buf[i] * g2 + b2
        mx[2 + i // 8, 1 + i % 8] = (inner * sigmoid(inner)).astype(BF16)
        return carry

    lax.fori_loop(0, 16, act_two, 0)
    halo_send(ACT)
    reduce_send(2, 1, merge_sums(2, 0))
    halo_wait(ACT)
    fill_narrow(lhs_a, ACT, False)
    reduce_send(2, 2, merge_sums(2, 1))
    block_out[...] = fx[pl.ds(2, 2), pl.ds(1, 8)] + convolve(lhs_a, 1, False)
    halo_wait(HID)
    halo_wait(GRAD)
    sums_2 = merge_sums(2, 2)
    norm_grads[2:4, :] = sums_2
    members = float(CELLS * N**3 * GROUP)
    both = group_sum(sums_2 * g2) * (1.0 / members)
    first_2, second_2 = both[1:2], both[0:1]

    def grad_hidden(v, g):
        unit = (v - centre_2) * inv_2
        inner = unit * g2 + b2
        s = sigmoid(inner)
        gi = g * s * (1.0 + inner * (1.0 - s))
        return (gi * g2 - first_2 - unit * second_2) * inv_2

    fill(lhs_b, [(hx, hk, hq), (gx, gk, gq)], True, ta < N - 1, grad_hidden, True)
    grad_act = convolve(lhs_b, 0, True)
    ga[...] = grad_act

    reduce_send(3, 0, back_sums(fx, 2, lambda t, h: ga[t, h], centre_1, inv_1, g1, b1))
    for field in (FEAT, COT, HID, ACT):
        halo_done(field)
    reduce_send(3, 1, merge_sums(3, 0))
    for conv in (0, 1):
        weights_done(conv)
    reduce_send(3, 2, merge_sums(3, 1))
    halo_done(GRAD)
    sums_1 = merge_sums(3, 2)
    norm_grads[0:2, :] = sums_1
    both = group_sum(sums_1 * g1) * (1.0 / members)
    first_1, second_1 = both[1:2], both[0:1]

    def last(i, carry):
        t, h = i // 8, i % 8
        field = (inner_grad[i] * g1 - first_1 - unit_buf[i] * second_1) * inv_1
        grad_input[t, h] = cx[t, h] + field
        return carry

    lax.fori_loop(0, 16, last, 0)
    for k in range(4):
        for s in range(3):
            for copy in reduce_copies(k, s):
                copy.wait_send()


def shards(features, cotangent, conv_one, conv_two, gain_one, bias_one, gain_two, bias_two):
    vmem = pl.BlockSpec(memory_space=pltpu.VMEM)
    anywhere = pl.BlockSpec(memory_space=pl.ANY)

    def buf(*shape, dtype=F32):
        return pltpu.VMEM(shape, dtype)

    scratch = (
        [buf(2, 8, 16, C)]
        + [buf(4, 10, 16, C)] * 3
        + [buf(4, 10, 16, C, dtype=BF16)] * 2
        + [buf(2, 4, 8, C)] * 3
        + [buf(2, 2, 16, C, dtype=BF16)] * 2
        + [buf(2, 2, 4, 1, C)] * 3
        + [buf(2, 2, 2, 16, C, dtype=BF16)] * 2
        + [buf(3, 2, 2, 8, C), buf(3, 2, 2, 2, 1, C)]
        + [buf(2, 2, 16, C, dtype=BF16), buf(2, 2, 2, 16, C, dtype=BF16)]
        + [buf(4, 10, 16, 3 * C, dtype=BF16)] * 2
        + [buf(2, N, 2, 2, 4, 7, 16, C // 2, dtype=BF16)]
        + [buf(2, 3, 144, 16, C, dtype=BF16)]
        + [buf(4, 3, 2, C), buf(4, 3, N, 2, C)]
        + [buf(16, 16, C)] * 2
        + [buf(2, 8, 16, C)]
        + [pltpu.SemaphoreType.DMA((2,))]
        + [pltpu.SemaphoreType.DMA((4, 3))] * 2
        + [pltpu.SemaphoreType.DMA((5, 27))] * 2
        + [pltpu.SemaphoreType.DMA((2, N))] * 4
        + [pltpu.SemaphoreType.DMA((2, N, 2))] * 2
        + [pltpu.SemaphoreType.DMA((2, N))] * 2
    )
    block = jax.ShapeDtypeStruct((2, 8, 16, C), F32)
    return pl.pallas_call(
        kernel,
        out_shape=(block, block, jax.ShapeDtypeStruct((4, C), F32)),
        in_specs=[anywhere] * 2 + [vmem] * 6,
        out_specs=(vmem, vmem, vmem),
        scratch_shapes=scratch,
        compiler_params=pltpu.CompilerParams(
            collective_id=0, has_side_effects=True, vmem_limit_bytes=56 * 2**20
        ),
    )(
        features, cotangent, conv_one, conv_two,
        gain_one[None], bias_one[None], gain_two[None], bias_two[None],
    )


def solution(mesh):
    return jax.shard_map(
        shards,
        mesh=mesh,
        in_specs=(
            P("ta", "ha", "wa", None),
            P("ta", "ha", "wa", None),
            P(None, ("ha", "wa"), None),
            P(None, ("ha", "wa"), None),
            P(),
            P(),
            P(),
            P(),
        ),
        out_specs=(P("ta", "ha", "wa", None), P("ta", "ha", "wa", None), P()),
        check_vma=False,
    )
```

```python
import functools

import jax
import jax.numpy as jnp
from jax import lax
from jax.experimental import pallas as pl
from jax.experimental.pallas import tpu as pltpu
from jax.sharding import PartitionSpec as P

AXES = ("ta", "ha", "wa")
N = 8
C = 256
GROUP = 8
NEAR = (1, 7, 2, 6, 3, 5, 4)
ORDER = ((0, 2, 1), (2, 1, 0), (2, 1, 0), (2, 1, 0))
EPS = 1e-06
CELLS = 256
MESH = pl.DeviceIdType.MESH
F32 = jnp.float32
BF16 = jnp.bfloat16

FEAT, HID, GRAD, COT, ACT = range(5)
NARROW = (COT, ACT)
OWN = {FEAT: 2, HID: 0, GRAD: 0, COT: 0, ACT: 2}


def sigmoid(v):
    return 1.0 / (1.0 + jnp.exp(-v))


def group_sum(v):
    lane = lax.broadcasted_iota(jnp.int32, v.shape, 1)
    for s in (1, 2, 4):
        up = pltpu.roll(v, s, 1)
        down = pltpu.roll(v, C - s, 1)
        v = v + jnp.where((lane & s) != 0, up, down)
    return v


def kernel(
    feat, cot, w_one, w_two, gain_one, bias_one, gain_two, bias_two,
    block_out, grad_input, norm_grads,
    cx, fx, hx, gx, nx, mx, fk, hk, gk, nk, mk, fq, hq, gq, nq, mq, ks, qs, ns, ms,
    lhs_a, lhs_b, shards_in, wb, stage, board, inner_grad, unit_buf, ga,
    local_sem, ar_s, ar_r, halo_s, halo_r, y_s, y_r, x_s, x_r, z_s, z_r, c_s, c_r,
):
    ta, ha, wa = (lax.axis_index(a) for a in AXES)
    me = (ta, ha, wa)
    core = lax.rem(wa, 2)
    sibling = (ta, ha, wa + 1 - 2 * core)
    fields = {FEAT: fx, HID: hx, GRAD: gx, COT: nx, ACT: mx}
    cols = {FEAT: fk, HID: hk, GRAD: gk, COT: nk, ACT: mk}
    corners = {FEAT: fq, HID: hq, GRAD: gq, COT: nq, ACT: mq}

    def along(axis, k):
        spot = list(me)
        spot[axis] = lax.rem(me[axis] + k, N)
        return tuple(spot)

    barrier = pltpu.get_barrier_semaphore()
    count = 0
    for axis in range(3):
        for k in range(1, N):
            pl.semaphore_signal(barrier, inc=1, device_id=along(axis, k), device_id_type=MESH)
            count += 1
    for dt in (-1, 0, 1):
        for dh in (-1, 0, 1):
            for dw in (-1, 0, 1):
                if abs(dt) + abs(dh) + abs(dw) >= 2:
                    spot = tuple(lax.rem(m + d + N, N) for m, d in zip(me, (dt, dh, dw)))
                    pl.semaphore_signal(barrier, inc=1, device_id=spot, device_id_type=MESH)
                    count += 1

    load_f = pltpu.make_async_copy(feat, fx.at[pl.ds(2, 2), pl.ds(1, 8)], local_sem.at[0])
    load_c = pltpu.make_async_copy(cot, cx, local_sem.at[1])
    load_f.start()
    load_c.start()

    def reduce_copies(k, s):
        axis = ORDER[k][s]
        return [
            pltpu.make_async_remote_copy(
                src_ref=stage.at[k, s],
                dst_ref=board.at[k, s, me[axis]],
                send_sem=ar_s.at[k, s],
                recv_sem=ar_r.at[k, s],
                device_id=along(axis, j),
                device_id_type=MESH,
            )
            for j in (4, 3, 5, 2, 6, 1, 7)
        ]

    def reduce_send(k, s, value):
        stage[k, s] = value
        board[k, s, me[ORDER[k][s]]] = value
        for copy in reduce_copies(k, s):
            copy.start()

    def reduce_get(k, s):
        seven = board.at[k, s, pl.ds(0, N - 1)]
        pltpu.make_async_copy(seven, seven, ar_r.at[k, s]).wait()
        return board[k, s]

    def merge_moments(k, s):
        got = reduce_get(k, s)
        cells = float(CELLS * N**s)
        means, squares = got[:, 0:1, :], got[:, 1:2, :]
        mean = jnp.sum(means, axis=0) * (1.0 / N)
        off = means - mean[None]
        square = jnp.sum(squares, axis=0) + cells * jnp.sum(off * off, axis=0)
        return jnp.concatenate([mean, square], axis=0)

    def merge_sums(k, s):
        return jnp.sum(reduce_get(k, s), axis=0)

    def local_moments(ref, own):
        v = ref[pl.ds(own, 2), pl.ds(1, 8)].reshape(CELLS, C)
        mean = jnp.sum(v, axis=0, keepdims=True) * (1.0 / CELLS)
        d = v - mean
        return jnp.concatenate([mean, jnp.sum(d * d, axis=0, keepdims=True)], axis=0)

    def finish_moments(pair):
        cells = float(CELLS * N**3)
        mean, square = pair[0:1], pair[1:2]
        centre = group_sum(mean) * (1.0 / GROUP)
        off = mean - centre
        spread = group_sum(square + cells * off * off) * (1.0 / (cells * GROUP))
        return centre, 1.0 / jnp.sqrt(spread + EPS)

    def halo_messages(field):
        own, x, k, q = OWN[field], fields[field], cols[field], corners[field]
        src_t = pl.ds(own, 2)
        narrow = field in NARROW
        for dt in (0, 1 if own else -1):
            dst_t = pl.ds(own - 2 * dt, 2)
            dst_k = (own - 2 * dt) // 2 if narrow else dst_t
            for dh in (0, -1, 1):
                for dw in (0, -1, 1):
                    if (dt, dh, dw) == (0, 0, 0):
                        continue
                    r, b = int(dw > 0), int(dh > 0)
                    if dh == 0 and dw == 0:
                        src, dst = x.at[src_t, pl.ds(1, 8)], x.at[dst_t, pl.ds(1, 8)]
                    elif dw == 0:
                        src, dst = x.at[src_t, 8 if b else 1], x.at[dst_t, 0 if b else 9]
                    elif dh == 0:
                        src = ns.at[field - COT, r] if narrow else ks.at[field, r]
                        dst = k.at[1 - r, dst_k]
                    else:
                        src = ms.at[field - COT, r, b] if narrow else qs.at[field, r, b]
                        dst = q.at[1 - r, 1 - b, dst_k]
                    spot = (ta + dt, ha + dh, wa + dw)
                    back = (ta - dt, ha - dh, wa - dw)
                    number = (dt + 1) * 9 + (dh + 1) * 3 + dw + 1
                    copy = pltpu.make_async_remote_copy(
                        src_ref=src, dst_ref=dst,
                        send_sem=halo_s.at[field, number], recv_sem=halo_r.at[field, number],
                        device_id=spot, device_id_type=MESH,
                    )
                    yield copy, inside(spot, (dt, dh, dw)), inside(back, (-dt, -dh, -dw))

    def inside(spot, delta):
        ok = None
        for v, d in zip(spot, delta):
            if d:
                one = v < N if d > 0 else v >= 0
                ok = one if ok is None else jnp.logical_and(ok, one)
        return ok

    def halo_send(field):
        own, x = OWN[field], fields[field]
        for r, w in ((0, 0), (1, 15)):
            if field in NARROW:
                ns[field - COT, r] = x[own : own + 2, 1:9, w, :].astype(F32).reshape(16, C).astype(BF16)
                for b, h in ((0, 1), (1, 8)):
                    pair = [x[own + t, h, w : w + 1, :].astype(F32) for t in range(2)]
                    ms[field - COT, r, b] = jnp.concatenate(pair + [jnp.zeros((14, C), F32)], axis=0).astype(BF16)
                continue
            for t in range(2):
                for h in range(8):
                    row = x[own + t, 1 + h, w : w + 1, :]
                    ks[field, r, t, h : h + 1, :] = row
                    if h in (0, 7):
                        qs[field, r, h // 7, t] = row
        for copy, goes, _ in halo_messages(field):
            pl.when(goes)(copy.start)

    def halo_wait(field):
        for copy, _, comes in halo_messages(field):
            pl.when(comes)(copy.wait_recv)

    def halo_done(field):
        for copy, goes, _ in halo_messages(field):
            pl.when(goes)(copy.wait_send)

    shift = 4 * lax.rem(wa, 4)
    half = lax.rem(ta, 2)
    column = lax.div(wa, 2)

    def block(j):
        return lax.rem(ha - j + N, N)

    row_half = lax.broadcasted_iota(jnp.int32, (16, C // 2), 0)

    def shard_stage(conv, ref):
        spare = None
        for a in range(3):
            rows = jnp.concatenate([ref[a].astype(F32), jnp.zeros((12, C), F32)], axis=0)
            rows = pltpu.roll(rows, shift, 0)
            rows = jnp.where(half == 0, rows[:, : C // 2], rows[:, C // 2 :])
            first, middle, end = rows[0:16], rows[16:32], rows[32:48]
            shards_in[conv, ha, core, half, column, 2 * a] = jnp.where(row_half >= shift, first, end).astype(BF16)
            shards_in[conv, ha, core, half, column, 2 * a + 1] = middle.astype(BF16)
            end = pltpu.roll(end, lax.rem(4 * a - shift + 16, 16), 0)
            spare = end if a == 0 else jnp.where(row_half >= 4 * a, end, spare)
        shards_in[conv, ha, core, half, column, 6] = spare.astype(BF16)

    def weight_copy(ref, sems, spot, device):
        return pltpu.make_async_remote_copy(
            src_ref=ref, dst_ref=ref, send_sem=sems[0].at[spot], recv_sem=sems[1].at[spot],
            device_id=device, device_id_type=MESH,
        )

    def along_ha(conv):
        ref = shards_in.at[conv, ha, core, half, column]
        return [weight_copy(ref, (y_s, y_r), (conv, j), along(1, j)) for j in NEAR]

    def along_wa(conv, j):
        ref = shards_in.at[conv, block(j), core, half, column]
        return [weight_copy(ref, (x_s, x_r), (conv, j), along(2, k)) for k in (2, 6, 4)]

    def along_ta(conv, j):
        ref = shards_in.at[conv, block(j), core, half]
        return [
            weight_copy(ref.at[pl.ds(0, 2)], (z_s, z_r), (conv, j, 0), along(0, 1)),
            weight_copy(ref.at[pl.ds(2, 2)], (z_s, z_r), (conv, j, 1), along(0, N - 1)),
        ]

    def across(conv, j):
        return [weight_copy(shards_in.at[conv, block(j), core], (c_s, c_r), (conv, j), sibling)]

    def start(copies):
        for copy in copies:
            copy.start()

    def arrived(ref, sem):
        pltpu.make_async_copy(ref, ref, sem).wait()

    def from_ha(conv, j):
        arrived(shards_in.at[conv, block(j), core, half, 0], y_r.at[conv, j])
        start(along_wa(conv, j))

    def from_wa(conv, j):
        arrived(shards_in.at[conv, block(j), core, half, pl.ds(0, 3)], x_r.at[conv, j])
        start(along_ta(conv, j))

    def from_ta(conv, j):
        ref = shards_in.at[conv, block(j), core, 1 - half]
        arrived(ref.at[pl.ds(0, 2)], z_r.at[conv, j, 0])
        arrived(ref.at[pl.ds(2, 2)], z_r.at[conv, j, 1])
        start(across(conv, j))

    def from_sibling(conv, j):
        arrived(shards_in.at[conv, block(j), 1 - core], c_r.at[conv, j])
        spot = block(j)

        def merge(g, carry):
            for s in range(2):
                def tile(p, i):
                    return shards_in[conv, spot, p % 2, s, 2 * g + p // 2, i].astype(F32)

                spare = [tile(p, 6) for p in range(4)]
                for a in range(3):
                    heads = [tile(p, 2 * a) for p in range(4)]
                    tiles = [heads[0]]
                    for p in range(4):
                        tiles.append(tile(p, 2 * a + 1))
                        end = pltpu.roll(spare[p], (4 * (p - a)) % 16, 0) if p != a else spare[p]
                        if p < 3:
                            end = jnp.where(row_half < 4 * p + 4, end, heads[p + 1])
                        tiles.append(jnp.where(row_half < 4 * p, heads[p], end) if p else end)
                    for i, value in enumerate(tiles):
                        wb[conv, a, 18 * spot + 9 * g + i, :, s * (C // 2) : (s + 1) * (C // 2)] = value.astype(BF16)
            return carry

        lax.fori_loop(0, 2, merge, 0)

    def weights_done(conv):
        copies = along_ha(conv)
        for j in range(N):
            copies += along_wa(conv, j) + along_ta(conv, j) + across(conv, j)
        for copy in copies:
            copy.wait_send()

    row_of = lax.broadcasted_iota(jnp.int32, (16, C), 0)

    top, bottom, left, right = ha > 0, ha < N - 1, wa > 0, wa < N - 1

    def put(lhs, t, h, v, before, after, flip):
        before = jnp.where(row_of == 0, before, pltpu.roll(v, 1, 0))
        after = jnp.where(row_of == 15, after, pltpu.roll(v, 15, 0))
        if flip:
            before, after = after, before
        lhs[t, h, :, 0:C] = before.astype(BF16)
        lhs[t, h, :, C : 2 * C] = v.astype(BF16)
        lhs[t, h, :, 2 * C : 3 * C] = after.astype(BF16)

    def fill_frame(lhs, t, frame, cell, side, corner, flip):
        edges = []
        for r, ok in ((0, left), (1, right)):
            ok = jnp.logical_and(ok, frame)
            mid = jnp.where(ok, side(r), 0.0)
            hi = jnp.where(jnp.logical_and(ok, top), corner(r, 0), 0.0)
            lo = jnp.where(jnp.logical_and(ok, bottom), corner(r, 1), 0.0)
            edges.append([hi] + [mid[h : h + 1] for h in range(8)] + [lo])
        for h in range(10):
            ok = frame
            if h == 0:
                ok = jnp.logical_and(ok, top)
            if h == 9:
                ok = jnp.logical_and(ok, bottom)
            put(lhs, t, h, jnp.where(ok, cell(h), 0.0), edges[0][h], edges[1][h], flip)

    def fill(lhs, refs, early, late, fn, flip):
        def body(t, carry):
            frame = jnp.logical_and(jnp.logical_or(t >= 2, early), jnp.logical_or(t < 2, late))
            fill_frame(
                lhs, t, frame,
                lambda h: fn(*[x[t, h] for x, _, _ in refs]),
                lambda r: fn(*[k[r, t] for _, k, _ in refs]),
                lambda r, b: fn(*[q[r, b, t] for _, _, q in refs]),
                flip,
            )
            return carry

        lax.fori_loop(0, 4, body, 0)

    def fill_narrow(lhs, field, flip):
        x, k, q, own = fields[field], cols[field], corners[field], OWN[field] // 2
        for t in range(4):
            w, u = t // 2, t % 2
            frame = True if w == own else (ta > 0 if own else ta < N - 1)
            fill_frame(
                lhs, t, frame,
                lambda h: x[t, h].astype(F32),
                lambda r: k[r, w].astype(F32)[8 * u : 8 * u + 8],
                lambda r, b: q[r, b, w].astype(F32)[u : u + 1],
                flip,
            )

    def convolve(lhs, conv, flip):
        total = None
        for a in range(3):
            for b in range(3):
                part = lhs[a : a + 2, b : b + 8].reshape(CELLS, 3 * C)
                if flip:
                    w = wb[conv, 2 - a, pl.ds(48 * (2 - b), 48)].reshape(3 * C, C)
                    out = None
                    for c in range(3):
                        one = lax.dot_general(
                            part[:, c * C : c * C + C], w[c * C : c * C + C, :],
                            (((1,), (1,)), ((), ())), preferred_element_type=F32,
                        )
                        out = one if out is None else out + one
                else:
                    w = wb[conv, a, pl.ds(48 * b, 48)].reshape(3 * C, C)
                    out = jnp.dot(part, w, preferred_element_type=F32)
                total = out if total is None else total + out
        return total.reshape(2, 8, 16, C)

    shard_stage(0, w_one)
    shard_stage(1, w_two)
    load_f.wait()
    moments = local_moments(fx, 2)
    pl.semaphore_wait(barrier, count)
    reduce_send(0, 0, moments)
    start(along_ha(0))
    start(along_wa(0, 0))
    halo_send(FEAT)
    start(along_ha(1))
    from_ha(0, 1)
    from_ha(0, 7)
    from_wa(0, 0)
    from_ha(0, 2)
    from_ha(0, 6)
    reduce_send(0, 1, merge_moments(0, 0))
    from_wa(0, 1)
    from_ha(0, 3)
    from_ha(0, 5)
    from_wa(0, 7)
    from_ha(0, 4)
    start(along_wa(1, 0))
    from_ha(1, 1)
    from_ta(0, 0)
    from_wa(0, 2)
    reduce_send(0, 2, merge_moments(0, 1))
    for j, k, m in ((1, 6, 7), (7, 3, 2), (2, 5, 6), (6, 4, 3)):
        from_ta(0, j)
        from_wa(0, k)
        from_ha(1, m)
    from_ha(1, 5)
    from_ha(1, 4)
    load_c.wait()
    nx[pl.ds(0, 2), pl.ds(1, 8)] = cx[...].astype(BF16)
    centre_1, inv_1 = finish_moments(merge_moments(0, 2))
    g1, b1, g2, b2 = gain_one[...], bias_one[...], gain_two[...], bias_two[...]
    halo_wait(FEAT)

    def act_one(v):
        inner = (v - centre_1) * inv_1 * g1 + b1
        return inner * sigmoid(inner)

    fill(lhs_a, [(fx, fk, fq)], ta > 0, True, act_one, False)
    halo_send(COT)
    for j in (0, 1, 7, 2):
        from_sibling(0, j)
    from_ta(0, 3)
    from_wa(1, 0)
    from_ta(0, 5)
    from_sibling(0, 6)
    from_ta(0, 4)
    from_wa(1, 1)
    from_sibling(0, 3)
    from_wa(1, 7)
    from_sibling(0, 5)
    from_sibling(0, 4)

    hx[pl.ds(0, 2), pl.ds(1, 8)] = convolve(lhs_a, 0, False)
    reduce_send(1, 0, local_moments(hx, 0))
    for j, k in ((2, 0), (6, 1), (3, 7)):
        from_wa(1, j)
        from_ta(1, k)
    reduce_send(1, 1, merge_moments(1, 0))
    for j, k in ((5, 2), (4, 6)):
        from_wa(1, j)
        from_ta(1, k)
    for j, k in ((3, 0), (5, 1), (4, 7)):
        from_ta(1, j)
        from_sibling(1, k)
    reduce_send(1, 2, merge_moments(1, 1))
    halo_send(HID)
    for j in (2, 6, 3, 5, 4):
        from_sibling(1, j)
    halo_wait(COT)
    fill_narrow(lhs_b, COT, True)
    gx[pl.ds(0, 2), pl.ds(1, 8)] = convolve(lhs_b, 1, True)
    halo_send(GRAD)
    centre_2, inv_2 = finish_moments(merge_moments(1, 2))

    def back_sums(field, own, grad, centre, inv, gain, bias):
        def body(i, carry):
            gain_sum, bias_sum = carry
            t, h = i // 8, i % 8
            unit = (field[own + t, 1 + h] - centre) * inv
            inner = unit * gain + bias
            s = sigmoid(inner)
            gi = grad(t, h) * s * (1.0 + inner * (1.0 - s))
            inner_grad[i] = gi
            unit_buf[i] = unit
            return gain_sum + gi * unit, bias_sum + gi

        zero = jnp.zeros((16, C), F32)
        sums = lax.fori_loop(0, 16, body, (zero, zero))
        return jnp.concatenate([jnp.sum(s, axis=0, keepdims=True) for s in sums], axis=0)

    reduce_send(2, 0, back_sums(hx, 0, lambda t, h: gx[t, 1 + h], centre_2, inv_2, g2, b2))

    def act_two(i, carry):
        inner = unit_buf[i] * g2 + b2
        mx[2 + i // 8, 1 + i % 8] = (inner * sigmoid(inner)).astype(BF16)
        return carry

    lax.fori_loop(0, 16, act_two, 0)
    halo_send(ACT)
    reduce_send(2, 1, merge_sums(2, 0))
    halo_wait(ACT)
    fill_narrow(lhs_a, ACT, False)
    reduce_send(2, 2, merge_sums(2, 1))
    block_out[...] = fx[pl.ds(2, 2), pl.ds(1, 8)] + convolve(lhs_a, 1, False)
    halo_wait(HID)
    halo_wait(GRAD)
    sums_2 = merge_sums(2, 2)
    norm_grads[2:4, :] = sums_2
    members = float(CELLS * N**3 * GROUP)
    both = group_sum(sums_2 * g2) * (1.0 / members)
    first_2, second_2 = both[1:2], both[0:1]

    def grad_hidden(v, g):
        unit = (v - centre_2) * inv_2
        inner = unit * g2 + b2
        s = sigmoid(inner)
        gi = g * s * (1.0 + inner * (1.0 - s))
        return (gi * g2 - first_2 - unit * second_2) * inv_2

    fill(lhs_b, [(hx, hk, hq), (gx, gk, gq)], True, ta < N - 1, grad_hidden, True)
    grad_act = convolve(lhs_b, 0, True)
    ga[...] = grad_act

    reduce_send(3, 0, back_sums(fx, 2, lambda t, h: ga[t, h], centre_1, inv_1, g1, b1))
    for field in (FEAT, COT, HID, ACT):
        halo_done(field)
    reduce_send(3, 1, merge_sums(3, 0))
    for conv in (0, 1):
        weights_done(conv)
    reduce_send(3, 2, merge_sums(3, 1))
    halo_done(GRAD)
    sums_1 = merge_sums(3, 2)
    norm_grads[0:2, :] = sums_1
    both = group_sum(sums_1 * g1) * (1.0 / members)
    first_1, second_1 = both[1:2], both[0:1]

    def last(i, carry):
        t, h = i // 8, i % 8
        field = (inner_grad[i] * g1 - first_1 - unit_buf[i] * second_1) * inv_1
        grad_input[t, h] = cx[t, h] + field
        return carry

    lax.fori_loop(0, 16, last, 0)
    for k in range(4):
        for s in range(3):
            for copy in reduce_copies(k, s):
                copy.wait_send()


def write_out(*refs):
    sems = refs[6]
    copies = [pltpu.make_async_copy(refs[i], refs[3 + i], sems.at[i]) for i in range(3)]
    for copy in copies:
        copy.start()
    for copy in copies:
        copy.wait()


def shards(features, cotangent, conv_one, conv_two, gain_one, bias_one, gain_two, bias_two):
    vmem = pl.BlockSpec(memory_space=pltpu.VMEM)
    anywhere = pl.BlockSpec(memory_space=pl.ANY)

    def buf(*shape, dtype=F32):
        return pltpu.VMEM(shape, dtype)

    scratch = (
        [buf(2, 8, 16, C)]
        + [buf(4, 10, 16, C)] * 3
        + [buf(4, 10, 16, C, dtype=BF16)] * 2
        + [buf(2, 4, 8, C)] * 3
        + [buf(2, 2, 16, C, dtype=BF16)] * 2
        + [buf(2, 2, 4, 1, C)] * 3
        + [buf(2, 2, 2, 16, C, dtype=BF16)] * 2
        + [buf(3, 2, 2, 8, C), buf(3, 2, 2, 2, 1, C)]
        + [buf(2, 2, 16, C, dtype=BF16), buf(2, 2, 2, 16, C, dtype=BF16)]
        + [buf(4, 10, 16, 3 * C, dtype=BF16)] * 2
        + [buf(2, N, 2, 2, 4, 7, 16, C // 2, dtype=BF16)]
        + [buf(2, 3, 144, 16, C, dtype=BF16)]
        + [buf(4, 3, 2, C), buf(4, 3, N, 2, C)]
        + [buf(16, 16, C)] * 2
        + [buf(2, 8, 16, C)]
        + [pltpu.SemaphoreType.DMA((2,))]
        + [pltpu.SemaphoreType.DMA((4, 3))] * 2
        + [pltpu.SemaphoreType.DMA((5, 27))] * 2
        + [pltpu.SemaphoreType.DMA((2, N))] * 4
        + [pltpu.SemaphoreType.DMA((2, N, 2))] * 2
        + [pltpu.SemaphoreType.DMA((2, N))] * 2
    )
    sizes = ((2, 8, 16, C), (2, 8, 16, C), (4, C))
    results = pl.pallas_call(
        kernel,
        out_shape=tuple(pltpu.VMEM(size, F32) for size in sizes),
        in_specs=[anywhere] * 2 + [vmem] * 6,
        out_specs=(vmem, vmem, vmem),
        scratch_shapes=scratch,
        compiler_params=pltpu.CompilerParams(
            collective_id=0, has_side_effects=True, vmem_limit_bytes=56 * 2**20
        ),
    )(
        features, cotangent, conv_one, conv_two,
        gain_one[None], bias_one[None], gain_two[None], bias_two[None],
    )
    return pl.pallas_call(
        write_out,
        out_shape=tuple(jax.ShapeDtypeStruct(size, F32) for size in sizes),
        in_specs=[vmem] * 3,
        out_specs=(anywhere,) * 3,
        scratch_shapes=[pltpu.SemaphoreType.DMA((3,))],
    )(*results)


def solution(mesh):
    return jax.shard_map(
        shards,
        mesh=mesh,
        in_specs=(
            P("ta", "ha", "wa", None),
            P("ta", "ha", "wa", None),
            P(None, ("ha", "wa"), None),
            P(None, ("ha", "wa"), None),
            P(),
            P(),
            P(),
            P(),
        ),
        out_specs=(P("ta", "ha", "wa", None), P("ta", "ha", "wa", None), P()),
        check_vma=False,
    )
```

```python
import functools

import jax
import jax.numpy as jnp
from jax import lax
from jax.experimental import pallas as pl
from jax.experimental.pallas import tpu as pltpu
from jax.sharding import PartitionSpec as P

AXES = ("ta", "ha", "wa")
N = 8
C = 256
GROUP = 8
NEAR = (1, 7, 2, 6, 3, 5, 4)
ORDER = ((0, 2, 1), (2, 1, 0), (2, 1, 0), (2, 1, 0))
EPS = 1e-06
CELLS = 256
MESH = pl.DeviceIdType.MESH
F32 = jnp.float32
BF16 = jnp.bfloat16

FEAT, HID, GRAD, COT, ACT = range(5)
NARROW = (COT, ACT)
OWN = {FEAT: 2, HID: 0, GRAD: 0, COT: 0, ACT: 2}


def sigmoid(v):
    return 1.0 / (1.0 + jnp.exp(-v))


def group_sum(v):
    lane = lax.broadcasted_iota(jnp.int32, v.shape, 1)
    for s in (1, 2, 4):
        up = pltpu.roll(v, s, 1)
        down = pltpu.roll(v, C - s, 1)
        v = v + jnp.where((lane & s) != 0, up, down)
    return v


def kernel(
    feat, cot, w_one, w_two, gain_one, bias_one, gain_two, bias_two,
    block_out, grad_input, norm_grads,
    cx, fx, hx, gx, nx, mx, fk, hk, gk, nk, mk, fq, hq, gq, nq, mq, ks, qs, ns, ms,
    lhs_a, lhs_b, shards_in, wb, stage, board, inner_grad, unit_buf, ga,
    local_sem, ar_s, ar_r, halo_s, halo_r, y_s, y_r, x_s, x_r, z_s, z_r, c_s, c_r,
):
    ta, ha, wa = (lax.axis_index(a) for a in AXES)
    me = (ta, ha, wa)
    core = lax.rem(wa, 2)
    sibling = (ta, ha, wa + 1 - 2 * core)
    fields = {FEAT: fx, HID: hx, GRAD: gx, COT: nx, ACT: mx}
    cols = {FEAT: fk, HID: hk, GRAD: gk, COT: nk, ACT: mk}
    corners = {FEAT: fq, HID: hq, GRAD: gq, COT: nq, ACT: mq}

    def along(axis, k):
        spot = list(me)
        spot[axis] = lax.rem(me[axis] + k, N)
        return tuple(spot)

    barrier = pltpu.get_barrier_semaphore()
    count = 0
    for axis in range(3):
        for k in range(1, N):
            pl.semaphore_signal(barrier, inc=1, device_id=along(axis, k), device_id_type=MESH)
            count += 1
    for dt in (-1, 0, 1):
        for dh in (-1, 0, 1):
            for dw in (-1, 0, 1):
                if abs(dt) + abs(dh) + abs(dw) >= 2:
                    spot = tuple(lax.rem(m + d + N, N) for m, d in zip(me, (dt, dh, dw)))
                    pl.semaphore_signal(barrier, inc=1, device_id=spot, device_id_type=MESH)
                    count += 1

    load_f = pltpu.make_async_copy(feat, fx.at[pl.ds(2, 2), pl.ds(1, 8)], local_sem.at[0])
    load_c = pltpu.make_async_copy(cot, cx, local_sem.at[1])
    load_f.start()
    load_c.start()

    def reduce_copies(k, s):
        axis = ORDER[k][s]
        return [
            pltpu.make_async_remote_copy(
                src_ref=stage.at[k, s],
                dst_ref=board.at[k, s, me[axis]],
                send_sem=ar_s.at[k, s],
                recv_sem=ar_r.at[k, s],
                device_id=along(axis, j),
                device_id_type=MESH,
            )
            for j in (4, 3, 5, 2, 6, 1, 7)
        ]

    def reduce_send(k, s, value):
        stage[k, s] = value
        board[k, s, me[ORDER[k][s]]] = value
        for copy in reduce_copies(k, s):
            copy.start()

    def reduce_get(k, s):
        seven = board.at[k, s, pl.ds(0, N - 1)]
        pltpu.make_async_copy(seven, seven, ar_r.at[k, s]).wait()
        return board[k, s]

    def merge_moments(k, s):
        got = reduce_get(k, s)
        cells = float(CELLS * N**s)
        means, squares = got[:, 0:1, :], got[:, 1:2, :]
        mean = jnp.sum(means, axis=0) * (1.0 / N)
        off = means - mean[None]
        square = jnp.sum(squares, axis=0) + cells * jnp.sum(off * off, axis=0)
        return jnp.concatenate([mean, square], axis=0)

    def merge_sums(k, s):
        return jnp.sum(reduce_get(k, s), axis=0)

    def local_moments(ref, own):
        v = ref[pl.ds(own, 2), pl.ds(1, 8)].reshape(CELLS, C)
        mean = jnp.sum(v, axis=0, keepdims=True) * (1.0 / CELLS)
        d = v - mean
        return jnp.concatenate([mean, jnp.sum(d * d, axis=0, keepdims=True)], axis=0)

    def finish_moments(pair):
        cells = float(CELLS * N**3)
        mean, square = pair[0:1], pair[1:2]
        centre = group_sum(mean) * (1.0 / GROUP)
        off = mean - centre
        spread = group_sum(square + cells * off * off) * (1.0 / (cells * GROUP))
        return centre, 1.0 / jnp.sqrt(spread + EPS)

    def halo_messages(field):
        own, x, k, q = OWN[field], fields[field], cols[field], corners[field]
        src_t = pl.ds(own, 2)
        narrow = field in NARROW
        for dt in (0, 1 if own else -1):
            dst_t = pl.ds(own - 2 * dt, 2)
            dst_k = (own - 2 * dt) // 2 if narrow else dst_t
            for dh in (0, -1, 1):
                for dw in (0, -1, 1):
                    if (dt, dh, dw) == (0, 0, 0):
                        continue
                    r, b = int(dw > 0), int(dh > 0)
                    if dh == 0 and dw == 0:
                        src, dst = x.at[src_t, pl.ds(1, 8)], x.at[dst_t, pl.ds(1, 8)]
                    elif dw == 0:
                        src, dst = x.at[src_t, 8 if b else 1], x.at[dst_t, 0 if b else 9]
                    elif dh == 0:
                        src = ns.at[field - COT, r] if narrow else ks.at[field, r]
                        dst = k.at[1 - r, dst_k]
                    else:
                        src = ms.at[field - COT, r, b] if narrow else qs.at[field, r, b]
                        dst = q.at[1 - r, 1 - b, dst_k]
                    spot = (ta + dt, ha + dh, wa + dw)
                    back = (ta - dt, ha - dh, wa - dw)
                    number = (dt + 1) * 9 + (dh + 1) * 3 + dw + 1
                    copy = pltpu.make_async_remote_copy(
                        src_ref=src, dst_ref=dst,
                        send_sem=halo_s.at[field, number], recv_sem=halo_r.at[field, number],
                        device_id=spot, device_id_type=MESH,
                    )
                    yield copy, inside(spot, (dt, dh, dw)), inside(back, (-dt, -dh, -dw))

    def inside(spot, delta):
        ok = None
        for v, d in zip(spot, delta):
            if d:
                one = v < N if d > 0 else v >= 0
                ok = one if ok is None else jnp.logical_and(ok, one)
        return ok

    def halo_send(field):
        own, x = OWN[field], fields[field]
        for r, w in ((0, 0), (1, 15)):
            if field in NARROW:
                ns[field - COT, r] = x[own : own + 2, 1:9, w, :].astype(F32).reshape(16, C).astype(BF16)
                for b, h in ((0, 1), (1, 8)):
                    pair = [x[own + t, h, w : w + 1, :].astype(F32) for t in range(2)]
                    ms[field - COT, r, b] = jnp.concatenate(pair + [jnp.zeros((14, C), F32)], axis=0).astype(BF16)
                continue
            for t in range(2):
                for h in range(8):
                    row = x[own + t, 1 + h, w : w + 1, :]
                    ks[field, r, t, h : h + 1, :] = row
                    if h in (0, 7):
                        qs[field, r, h // 7, t] = row
        for copy, goes, _ in halo_messages(field):
            pl.when(goes)(copy.start)

    def halo_wait(field):
        for copy, _, comes in halo_messages(field):
            pl.when(comes)(copy.wait_recv)

    def halo_done(field):
        for copy, goes, _ in halo_messages(field):
            pl.when(goes)(copy.wait_send)

    shift = 4 * lax.rem(wa, 4)
    half = lax.rem(ta, 2)
    column = lax.div(wa, 2)

    def block(j):
        return lax.rem(ha - j + N, N)

    row_half = lax.broadcasted_iota(jnp.int32, (16, C // 2), 0)

    def shard_stage(conv, ref):
        spare = None
        for a in range(3):
            rows = jnp.concatenate([ref[a].astype(F32), jnp.zeros((12, C), F32)], axis=0)
            rows = pltpu.roll(rows, shift, 0)
            rows = jnp.where(half == 0, rows[:, : C // 2], rows[:, C // 2 :])
            first, middle, end = rows[0:16], rows[16:32], rows[32:48]
            shards_in[conv, ha, core, half, column, 2 * a] = jnp.where(row_half >= shift, first, end).astype(BF16)
            shards_in[conv, ha, core, half, column, 2 * a + 1] = middle.astype(BF16)
            end = pltpu.roll(end, lax.rem(4 * a - shift + 16, 16), 0)
            spare = end if a == 0 else jnp.where(row_half >= 4 * a, end, spare)
        shards_in[conv, ha, core, half, column, 6] = spare.astype(BF16)

    def weight_copy(ref, sems, spot, device):
        return pltpu.make_async_remote_copy(
            src_ref=ref, dst_ref=ref, send_sem=sems[0].at[spot], recv_sem=sems[1].at[spot],
            device_id=device, device_id_type=MESH,
        )

    def along_ha(conv):
        ref = shards_in.at[conv, ha, core, half, column]
        return [weight_copy(ref, (y_s, y_r), (conv, j), along(1, j)) for j in NEAR]

    def along_wa(conv, j):
        ref = shards_in.at[conv, block(j), core, half, column]
        return [weight_copy(ref, (x_s, x_r), (conv, j), along(2, k)) for k in (2, 6, 4)]

    def along_ta(conv, j):
        ref = shards_in.at[conv, block(j), core, half]
        return [
            weight_copy(ref.at[pl.ds(0, 2)], (z_s, z_r), (conv, j, 0), along(0, 1)),
            weight_copy(ref.at[pl.ds(2, 2)], (z_s, z_r), (conv, j, 1), along(0, N - 1)),
        ]

    def across(conv, j):
        return [weight_copy(shards_in.at[conv, block(j), core], (c_s, c_r), (conv, j), sibling)]

    def start(copies):
        for copy in copies:
            copy.start()

    def arrived(ref, sem):
        pltpu.make_async_copy(ref, ref, sem).wait()

    def from_ha(conv, j):
        arrived(shards_in.at[conv, block(j), core, half, 0], y_r.at[conv, j])
        start(along_wa(conv, j))

    def from_wa(conv, j):
        arrived(shards_in.at[conv, block(j), core, half, pl.ds(0, 3)], x_r.at[conv, j])
        start(along_ta(conv, j))

    def from_ta(conv, j):
        ref = shards_in.at[conv, block(j), core, 1 - half]
        arrived(ref.at[pl.ds(0, 2)], z_r.at[conv, j, 0])
        arrived(ref.at[pl.ds(2, 2)], z_r.at[conv, j, 1])
        start(across(conv, j))

    def from_sibling(conv, j):
        arrived(shards_in.at[conv, block(j), 1 - core], c_r.at[conv, j])
        spot = block(j)

        def merge(g, carry):
            for s in range(2):
                def tile(p, i):
                    return shards_in[conv, spot, p % 2, s, 2 * g + p // 2, i].astype(F32)

                spare = [tile(p, 6) for p in range(4)]
                for a in range(3):
                    heads = [tile(p, 2 * a) for p in range(4)]
                    tiles = [heads[0]]
                    for p in range(4):
                        tiles.append(tile(p, 2 * a + 1))
                        end = pltpu.roll(spare[p], (4 * (p - a)) % 16, 0) if p != a else spare[p]
                        if p < 3:
                            end = jnp.where(row_half < 4 * p + 4, end, heads[p + 1])
                        tiles.append(jnp.where(row_half < 4 * p, heads[p], end) if p else end)
                    for i, value in enumerate(tiles):
                        wb[conv, a, 18 * spot + 9 * g + i, :, s * (C // 2) : (s + 1) * (C // 2)] = value.astype(BF16)
            return carry

        lax.fori_loop(0, 2, merge, 0)

    def weights_done(conv):
        copies = along_ha(conv)
        for j in range(N):
            copies += along_wa(conv, j) + along_ta(conv, j) + across(conv, j)
        for copy in copies:
            copy.wait_send()

    row_of = lax.broadcasted_iota(jnp.int32, (16, C), 0)

    top, bottom, left, right = ha > 0, ha < N - 1, wa > 0, wa < N - 1

    def put(lhs, t, h, v, before, after, flip):
        before = jnp.where(row_of == 0, before, pltpu.roll(v, 1, 0))
        after = jnp.where(row_of == 15, after, pltpu.roll(v, 15, 0))
        if flip:
            before, after = after, before
        lhs[t, h, :, 0:C] = before.astype(BF16)
        lhs[t, h, :, C : 2 * C] = v.astype(BF16)
        lhs[t, h, :, 2 * C : 3 * C] = after.astype(BF16)

    def fill_frame(lhs, t, frame, cell, side, corner, flip):
        edges = []
        for r, ok in ((0, left), (1, right)):
            ok = jnp.logical_and(ok, frame)
            mid = jnp.where(ok, side(r), 0.0)
            hi = jnp.where(jnp.logical_and(ok, top), corner(r, 0), 0.0)
            lo = jnp.where(jnp.logical_and(ok, bottom), corner(r, 1), 0.0)
            edges.append([hi] + [mid[h : h + 1] for h in range(8)] + [lo])
        for h in range(10):
            ok = frame
            if h == 0:
                ok = jnp.logical_and(ok, top)
            if h == 9:
                ok = jnp.logical_and(ok, bottom)
            put(lhs, t, h, jnp.where(ok, cell(h), 0.0), edges[0][h], edges[1][h], flip)

    def fill(lhs, refs, early, late, fn, flip):
        def body(t, carry):
            frame = jnp.logical_and(jnp.logical_or(t >= 2, early), jnp.logical_or(t < 2, late))
            fill_frame(
                lhs, t, frame,
                lambda h: fn(*[x[t, h] for x, _, _ in refs]),
                lambda r: fn(*[k[r, t] for _, k, _ in refs]),
                lambda r, b: fn(*[q[r, b, t] for _, _, q in refs]),
                flip,
            )
            return carry

        lax.fori_loop(0, 4, body, 0)

    def fill_narrow(lhs, field, flip):
        x, k, q, own = fields[field], cols[field], corners[field], OWN[field] // 2
        for t in range(4):
            w, u = t // 2, t % 2
            frame = True if w == own else (ta > 0 if own else ta < N - 1)
            fill_frame(
                lhs, t, frame,
                lambda h: x[t, h].astype(F32),
                lambda r: k[r, w].astype(F32)[8 * u : 8 * u + 8],
                lambda r, b: q[r, b, w].astype(F32)[u : u + 1],
                flip,
            )

    def convolve(lhs, conv, flip):
        total = None
        for a in range(3):
            for b in range(3):
                part = lhs[a : a + 2, b : b + 8].reshape(CELLS, 3 * C)
                if flip:
                    w = wb[conv, 2 - a, pl.ds(48 * (2 - b), 48)].reshape(3 * C, C)
                    out = None
                    for c in range(3):
                        one = lax.dot_general(
                            part[:, c * C : c * C + C], w[c * C : c * C + C, :],
                            (((1,), (1,)), ((), ())), preferred_element_type=F32,
                        )
                        out = one if out is None else out + one
                else:
                    w = wb[conv, a, pl.ds(48 * b, 48)].reshape(3 * C, C)
                    out = jnp.dot(part, w, preferred_element_type=F32)
                total = out if total is None else total + out
        return total.reshape(2, 8, 16, C)

    shard_stage(0, w_one)
    shard_stage(1, w_two)
    load_f.wait()
    moments = local_moments(fx, 2)
    pl.semaphore_wait(barrier, count)
    reduce_send(0, 0, moments)
    start(along_ha(0))
    start(along_wa(0, 0))
    halo_send(FEAT)
    start(along_ha(1))
    from_ha(0, 1)
    from_ha(0, 7)
    from_wa(0, 0)
    from_ha(0, 2)
    from_ha(0, 6)
    reduce_send(0, 1, merge_moments(0, 0))
    from_wa(0, 1)
    from_ha(0, 3)
    from_ha(0, 5)
    from_wa(0, 7)
    from_ha(0, 4)
    start(along_wa(1, 0))
    from_ha(1, 1)
    from_ta(0, 0)
    from_wa(0, 2)
    reduce_send(0, 2, merge_moments(0, 1))
    for j, k, m in ((1, 6, 7), (7, 3, 2), (2, 5, 6), (6, 4, 3)):
        from_ta(0, j)
        from_wa(0, k)
        from_ha(1, m)
    from_ha(1, 5)
    from_ha(1, 4)
    load_c.wait()
    nx[pl.ds(0, 2), pl.ds(1, 8)] = cx[...].astype(BF16)
    centre_1, inv_1 = finish_moments(merge_moments(0, 2))
    g1, b1, g2, b2 = gain_one[...], bias_one[...], gain_two[...], bias_two[...]
    halo_wait(FEAT)

    def act_one(v):
        inner = (v - centre_1) * inv_1 * g1 + b1
        return inner * sigmoid(inner)

    fill(lhs_a, [(fx, fk, fq)], ta > 0, True, act_one, False)
    halo_send(COT)
    for j in (0, 1, 7, 2):
        from_sibling(0, j)
    from_ta(0, 3)
    from_wa(1, 0)
    from_ta(0, 5)
    from_sibling(0, 6)
    from_ta(0, 4)
    from_wa(1, 1)
    from_sibling(0, 3)
    from_wa(1, 7)
    from_sibling(0, 5)
    from_sibling(0, 4)

    hx[pl.ds(0, 2), pl.ds(1, 8)] = convolve(lhs_a, 0, False)
    reduce_send(1, 0, local_moments(hx, 0))
    for j, k in ((2, 0), (6, 1), (3, 7)):
        from_wa(1, j)
        from_ta(1, k)
    reduce_send(1, 1, merge_moments(1, 0))
    for j, k in ((5, 2), (4, 6)):
        from_wa(1, j)
        from_ta(1, k)
    for j, k in ((3, 0), (5, 1), (4, 7)):
        from_ta(1, j)
        from_sibling(1, k)
    reduce_send(1, 2, merge_moments(1, 1))
    halo_send(HID)
    for j in (2, 6, 3, 5, 4):
        from_sibling(1, j)
    halo_wait(COT)
    fill_narrow(lhs_b, COT, True)
    gx[pl.ds(0, 2), pl.ds(1, 8)] = convolve(lhs_b, 1, True)
    halo_send(GRAD)
    centre_2, inv_2 = finish_moments(merge_moments(1, 2))

    def back_sums(field, own, grad, centre, inv, gain, bias):
        def body(i, carry):
            gain_sum, bias_sum = carry
            t, h = i // 8, i % 8
            unit = (field[own + t, 1 + h] - centre) * inv
            inner = unit * gain + bias
            s = sigmoid(inner)
            gi = grad(t, h) * s * (1.0 + inner * (1.0 - s))
            inner_grad[i] = gi
            unit_buf[i] = unit
            return gain_sum + gi * unit, bias_sum + gi

        zero = jnp.zeros((16, C), F32)
        sums = lax.fori_loop(0, 16, body, (zero, zero), unroll=8)
        return jnp.concatenate([jnp.sum(s, axis=0, keepdims=True) for s in sums], axis=0)

    reduce_send(2, 0, back_sums(hx, 0, lambda t, h: gx[t, 1 + h], centre_2, inv_2, g2, b2))

    def act_two(i, carry):
        inner = unit_buf[i] * g2 + b2
        mx[2 + i // 8, 1 + i % 8] = (inner * sigmoid(inner)).astype(BF16)
        return carry

    lax.fori_loop(0, 16, act_two, 0, unroll=4)
    halo_send(ACT)
    reduce_send(2, 1, merge_sums(2, 0))
    halo_wait(ACT)
    fill_narrow(lhs_a, ACT, False)
    reduce_send(2, 2, merge_sums(2, 1))
    block_out[...] = fx[pl.ds(2, 2), pl.ds(1, 8)] + convolve(lhs_a, 1, False)
    halo_wait(HID)
    halo_wait(GRAD)
    sums_2 = merge_sums(2, 2)
    norm_grads[2:4, :] = sums_2
    members = float(CELLS * N**3 * GROUP)
    both = group_sum(sums_2 * g2) * (1.0 / members)
    first_2, second_2 = both[1:2], both[0:1]

    def grad_hidden(v, g):
        unit = (v - centre_2) * inv_2
        inner = unit * g2 + b2
        s = sigmoid(inner)
        gi = g * s * (1.0 + inner * (1.0 - s))
        return (gi * g2 - first_2 - unit * second_2) * inv_2

    fill(lhs_b, [(hx, hk, hq), (gx, gk, gq)], True, ta < N - 1, grad_hidden, True)
    grad_act = convolve(lhs_b, 0, True)
    ga[...] = grad_act

    reduce_send(3, 0, back_sums(fx, 2, lambda t, h: ga[t, h], centre_1, inv_1, g1, b1))
    for field in (FEAT, COT, HID, ACT):
        halo_done(field)
    reduce_send(3, 1, merge_sums(3, 0))
    for conv in (0, 1):
        weights_done(conv)
    reduce_send(3, 2, merge_sums(3, 1))
    halo_done(GRAD)
    sums_1 = merge_sums(3, 2)
    norm_grads[0:2, :] = sums_1
    both = group_sum(sums_1 * g1) * (1.0 / members)
    first_1, second_1 = both[1:2], both[0:1]

    def last(i, carry):
        t, h = i // 8, i % 8
        field = (inner_grad[i] * g1 - first_1 - unit_buf[i] * second_1) * inv_1
        grad_input[t, h] = cx[t, h] + field
        return carry

    lax.fori_loop(0, 16, last, 0, unroll=8)
    for k in range(4):
        for s in range(3):
            for copy in reduce_copies(k, s):
                copy.wait_send()


def write_out(*refs):
    sems = refs[6]
    copies = [pltpu.make_async_copy(refs[i], refs[3 + i], sems.at[i]) for i in range(3)]
    for copy in copies:
        copy.start()
    for copy in copies:
        copy.wait()


def shards(features, cotangent, conv_one, conv_two, gain_one, bias_one, gain_two, bias_two):
    vmem = pl.BlockSpec(memory_space=pltpu.VMEM)
    anywhere = pl.BlockSpec(memory_space=pl.ANY)

    def buf(*shape, dtype=F32):
        return pltpu.VMEM(shape, dtype)

    scratch = (
        [buf(2, 8, 16, C)]
        + [buf(4, 10, 16, C)] * 3
        + [buf(4, 10, 16, C, dtype=BF16)] * 2
        + [buf(2, 4, 8, C)] * 3
        + [buf(2, 2, 16, C, dtype=BF16)] * 2
        + [buf(2, 2, 4, 1, C)] * 3
        + [buf(2, 2, 2, 16, C, dtype=BF16)] * 2
        + [buf(3, 2, 2, 8, C), buf(3, 2, 2, 2, 1, C)]
        + [buf(2, 2, 16, C, dtype=BF16), buf(2, 2, 2, 16, C, dtype=BF16)]
        + [buf(4, 10, 16, 3 * C, dtype=BF16)] * 2
        + [buf(2, N, 2, 2, 4, 7, 16, C // 2, dtype=BF16)]
        + [buf(2, 3, 144, 16, C, dtype=BF16)]
        + [buf(4, 3, 2, C), buf(4, 3, N, 2, C)]
        + [buf(16, 16, C)] * 2
        + [buf(2, 8, 16, C)]
        + [pltpu.SemaphoreType.DMA((2,))]
        + [pltpu.SemaphoreType.DMA((4, 3))] * 2
        + [pltpu.SemaphoreType.DMA((5, 27))] * 2
        + [pltpu.SemaphoreType.DMA((2, N))] * 4
        + [pltpu.SemaphoreType.DMA((2, N, 2))] * 2
        + [pltpu.SemaphoreType.DMA((2, N))] * 2
    )
    sizes = ((2, 8, 16, C), (2, 8, 16, C), (4, C))
    results = pl.pallas_call(
        kernel,
        out_shape=tuple(pltpu.VMEM(size, F32) for size in sizes),
        in_specs=[anywhere] * 2 + [vmem] * 6,
        out_specs=(vmem, vmem, vmem),
        scratch_shapes=scratch,
        compiler_params=pltpu.CompilerParams(
            collective_id=0, has_side_effects=True, vmem_limit_bytes=56 * 2**20
        ),
    )(
        features, cotangent, conv_one, conv_two,
        gain_one[None], bias_one[None], gain_two[None], bias_two[None],
    )
    return pl.pallas_call(
        write_out,
        out_shape=tuple(jax.ShapeDtypeStruct(size, F32) for size in sizes),
        in_specs=[vmem] * 3,
        out_specs=(anywhere,) * 3,
        scratch_shapes=[pltpu.SemaphoreType.DMA((3,))],
    )(*[pltpu.with_memory_space_constraint(r, pltpu.VMEM) for r in results])


def solution(mesh):
    return jax.shard_map(
        shards,
        mesh=mesh,
        in_specs=(
            P("ta", "ha", "wa", None),
            P("ta", "ha", "wa", None),
            P(None, ("ha", "wa"), None),
            P(None, ("ha", "wa"), None),
            P(),
            P(),
            P(),
            P(),
        ),
        out_specs=(P("ta", "ha", "wa", None), P("ta", "ha", "wa", None), P()),
        check_vma=False,
    )
```

```python
import functools

import jax
import jax.numpy as jnp
from jax import lax
from jax.experimental import pallas as pl
from jax.experimental.pallas import tpu as pltpu
from jax.sharding import PartitionSpec as P

AXES = ("ta", "ha", "wa")
N = 8
C = 256
GROUP = 8
NEAR = (1, 7, 2, 6, 3, 5, 4)
ORDER = ((0, 2, 1), (1, 2, 0), (1, 2, 0), (2, 1, 0))
EPS = 1e-06
CELLS = 256
MESH = pl.DeviceIdType.MESH
F32 = jnp.float32
BF16 = jnp.bfloat16

FEAT, HID, GRAD, COT, ACT = range(5)
NARROW = (COT, ACT)
OWN = {FEAT: 2, HID: 0, GRAD: 0, COT: 0, ACT: 2}


def sigmoid(v):
    return 1.0 / (1.0 + jnp.exp(-v))


def group_sum(v):
    lane = lax.broadcasted_iota(jnp.int32, v.shape, 1)
    for s in (1, 2, 4):
        up = pltpu.roll(v, s, 1)
        down = pltpu.roll(v, C - s, 1)
        v = v + jnp.where((lane & s) != 0, up, down)
    return v


def kernel(
    feat, cot, w_one, w_two, gain_one, bias_one, gain_two, bias_two,
    block_out, grad_input, norm_grads,
    cx, fx, hx, gx, nx, mx, fk, hk, gk, nk, mk, fq, hq, gq, nq, mq, ks, qs, ns, ms,
    lhs_a, lhs_b, shards_in, wb, stage, board, inner_grad, unit_buf, ga,
    local_sem, ar_s, ar_r, halo_s, halo_r, y_s, y_r, x_s, x_r, z_s, z_r, c_s, c_r,
):
    ta, ha, wa = (lax.axis_index(a) for a in AXES)
    me = (ta, ha, wa)
    core = lax.rem(wa, 2)
    sibling = (ta, ha, wa + 1 - 2 * core)
    fields = {FEAT: fx, HID: hx, GRAD: gx, COT: nx, ACT: mx}
    cols = {FEAT: fk, HID: hk, GRAD: gk, COT: nk, ACT: mk}
    corners = {FEAT: fq, HID: hq, GRAD: gq, COT: nq, ACT: mq}

    def along(axis, k):
        spot = list(me)
        spot[axis] = lax.rem(me[axis] + k, N)
        return tuple(spot)

    barrier = pltpu.get_barrier_semaphore()
    count = 0
    for axis in range(3):
        for k in range(1, N):
            pl.semaphore_signal(barrier, inc=1, device_id=along(axis, k), device_id_type=MESH)
            count += 1
    for dt in (-1, 0, 1):
        for dh in (-1, 0, 1):
            for dw in (-1, 0, 1):
                if abs(dt) + abs(dh) + abs(dw) >= 2:
                    spot = tuple(lax.rem(m + d + N, N) for m, d in zip(me, (dt, dh, dw)))
                    pl.semaphore_signal(barrier, inc=1, device_id=spot, device_id_type=MESH)
                    count += 1

    load_f = pltpu.make_async_copy(feat, fx.at[pl.ds(2, 2), pl.ds(1, 8)], local_sem.at[0])
    load_c = pltpu.make_async_copy(cot, cx, local_sem.at[1])
    load_f.start()
    load_c.start()

    def reduce_copies(k, s):
        axis = ORDER[k][s]
        return [
            pltpu.make_async_remote_copy(
                src_ref=stage.at[k, s],
                dst_ref=board.at[k, s, me[axis]],
                send_sem=ar_s.at[k, s],
                recv_sem=ar_r.at[k, s],
                device_id=along(axis, j),
                device_id_type=MESH,
            )
            for j in (4, 3, 5, 2, 6, 1, 7)
        ]

    def reduce_send(k, s, value):
        stage[k, s] = value
        board[k, s, me[ORDER[k][s]]] = value
        for copy in reduce_copies(k, s):
            copy.start()

    def reduce_get(k, s):
        seven = board.at[k, s, pl.ds(0, N - 1)]
        pltpu.make_async_copy(seven, seven, ar_r.at[k, s]).wait()
        return board[k, s]

    def merge_moments(k, s):
        got = reduce_get(k, s)
        cells = float(CELLS * N**s)
        means, squares = got[:, 0:1, :], got[:, 1:2, :]
        mean = jnp.sum(means, axis=0) * (1.0 / N)
        off = means - mean[None]
        square = jnp.sum(squares, axis=0) + cells * jnp.sum(off * off, axis=0)
        return jnp.concatenate([mean, square], axis=0)

    def merge_sums(k, s):
        return jnp.sum(reduce_get(k, s), axis=0)

    def local_moments(ref, own):
        v = ref[pl.ds(own, 2), pl.ds(1, 8)].reshape(CELLS, C)
        mean = jnp.sum(v, axis=0, keepdims=True) * (1.0 / CELLS)
        d = v - mean
        return jnp.concatenate([mean, jnp.sum(d * d, axis=0, keepdims=True)], axis=0)

    def finish_moments(pair):
        cells = float(CELLS * N**3)
        mean, square = pair[0:1], pair[1:2]
        centre = group_sum(mean) * (1.0 / GROUP)
        off = mean - centre
        spread = group_sum(square + cells * off * off) * (1.0 / (cells * GROUP))
        return centre, 1.0 / jnp.sqrt(spread + EPS)

    def halo_messages(field):
        own, x, k, q = OWN[field], fields[field], cols[field], corners[field]
        src_t = pl.ds(own, 2)
        narrow = field in NARROW
        for dt in (0, 1 if own else -1):
            dst_t = pl.ds(own - 2 * dt, 2)
            dst_k = (own - 2 * dt) // 2 if narrow else dst_t
            for dh in (0, -1, 1):
                for dw in (0, -1, 1):
                    if (dt, dh, dw) == (0, 0, 0):
                        continue
                    r, b = int(dw > 0), int(dh > 0)
                    if dh == 0 and dw == 0:
                        src, dst = x.at[src_t, pl.ds(1, 8)], x.at[dst_t, pl.ds(1, 8)]
                    elif dw == 0:
                        src, dst = x.at[src_t, 8 if b else 1], x.at[dst_t, 0 if b else 9]
                    elif dh == 0:
                        src = ns.at[field - COT, r] if narrow else ks.at[field, r]
                        dst = k.at[1 - r, dst_k]
                    else:
                        src = ms.at[field - COT, r, b] if narrow else qs.at[field, r, b]
                        dst = q.at[1 - r, 1 - b, dst_k]
                    spot = (ta + dt, ha + dh, wa + dw)
                    back = (ta - dt, ha - dh, wa - dw)
                    number = (dt + 1) * 9 + (dh + 1) * 3 + dw + 1
                    copy = pltpu.make_async_remote_copy(
                        src_ref=src, dst_ref=dst,
                        send_sem=halo_s.at[field, number], recv_sem=halo_r.at[field, number],
                        device_id=spot, device_id_type=MESH,
                    )
                    yield copy, inside(spot, (dt, dh, dw)), inside(back, (-dt, -dh, -dw))

    def inside(spot, delta):
        ok = None
        for v, d in zip(spot, delta):
            if d:
                one = v < N if d > 0 else v >= 0
                ok = one if ok is None else jnp.logical_and(ok, one)
        return ok

    def halo_send(field):
        own, x = OWN[field], fields[field]
        for r, w in ((0, 0), (1, 15)):
            if field in NARROW:
                ns[field - COT, r] = x[own : own + 2, 1:9, w, :].astype(F32).reshape(16, C).astype(BF16)
                for b, h in ((0, 1), (1, 8)):
                    pair = [x[own + t, h, w : w + 1, :].astype(F32) for t in range(2)]
                    ms[field - COT, r, b] = jnp.concatenate(pair + [jnp.zeros((14, C), F32)], axis=0).astype(BF16)
                continue
            for t in range(2):
                for h in range(8):
                    row = x[own + t, 1 + h, w : w + 1, :]
                    ks[field, r, t, h : h + 1, :] = row
                    if h in (0, 7):
                        qs[field, r, h // 7, t] = row
        for copy, goes, _ in halo_messages(field):
            pl.when(goes)(copy.start)

    def halo_wait(field):
        for copy, _, comes in halo_messages(field):
            pl.when(comes)(copy.wait_recv)

    def halo_done(field):
        for copy, goes, _ in halo_messages(field):
            pl.when(goes)(copy.wait_send)

    shift = 4 * lax.rem(wa, 4)
    half = lax.rem(ta, 2)
    column = lax.div(wa, 2)

    def block(j):
        return lax.rem(ha - j + N, N)

    row_half = lax.broadcasted_iota(jnp.int32, (16, C // 2), 0)

    def shard_stage(conv, ref):
        spare = None
        for a in range(3):
            rows = jnp.concatenate([ref[a].astype(F32), jnp.zeros((12, C), F32)], axis=0)
            rows = pltpu.roll(rows, shift, 0)
            rows = jnp.where(half == 0, rows[:, : C // 2], rows[:, C // 2 :])
            first, middle, end = rows[0:16], rows[16:32], rows[32:48]
            shards_in[conv, ha, core, half, column, 2 * a] = jnp.where(row_half >= shift, first, end).astype(BF16)
            shards_in[conv, ha, core, half, column, 2 * a + 1] = middle.astype(BF16)
            end = pltpu.roll(end, lax.rem(4 * a - shift + 16, 16), 0)
            spare = end if a == 0 else jnp.where(row_half >= 4 * a, end, spare)
        shards_in[conv, ha, core, half, column, 6] = spare.astype(BF16)

    def weight_copy(ref, sems, spot, device):
        return pltpu.make_async_remote_copy(
            src_ref=ref, dst_ref=ref, send_sem=sems[0].at[spot], recv_sem=sems[1].at[spot],
            device_id=device, device_id_type=MESH,
        )

    def along_ha(conv):
        ref = shards_in.at[conv, ha, core, half, column]
        return [weight_copy(ref, (y_s, y_r), (conv, j), along(1, j)) for j in NEAR]

    def along_wa(conv, j):
        ref = shards_in.at[conv, block(j), core, half, column]
        return [weight_copy(ref, (x_s, x_r), (conv, j), along(2, k)) for k in (2, 6, 4)]

    def along_ta(conv, j):
        ref = shards_in.at[conv, block(j), core, half]
        return [
            weight_copy(ref.at[pl.ds(0, 2)], (z_s, z_r), (conv, j, 0), along(0, 1)),
            weight_copy(ref.at[pl.ds(2, 2)], (z_s, z_r), (conv, j, 1), along(0, N - 1)),
        ]

    def across(conv, j):
        return [weight_copy(shards_in.at[conv, block(j), core], (c_s, c_r), (conv, j), sibling)]

    def start(copies):
        for copy in copies:
            copy.start()

    def arrived(ref, sem):
        pltpu.make_async_copy(ref, ref, sem).wait()

    def from_ha(conv, j):
        arrived(shards_in.at[conv, block(j), core, half, 0], y_r.at[conv, j])
        start(along_wa(conv, j))

    def from_wa(conv, j):
        arrived(shards_in.at[conv, block(j), core, half, pl.ds(0, 3)], x_r.at[conv, j])
        start(along_ta(conv, j))

    def from_ta(conv, j):
        ref = shards_in.at[conv, block(j), core, 1 - half]
        arrived(ref.at[pl.ds(0, 2)], z_r.at[conv, j, 0])
        arrived(ref.at[pl.ds(2, 2)], z_r.at[conv, j, 1])
        start(across(conv, j))

    def from_sibling(conv, j):
        arrived(shards_in.at[conv, block(j), 1 - core], c_r.at[conv, j])
        spot = block(j)

        def merge(g, carry):
            for s in range(2):
                def tile(p, i):
                    return shards_in[conv, spot, p % 2, s, 2 * g + p // 2, i].astype(F32)

                spare = [tile(p, 6) for p in range(4)]
                for a in range(3):
                    heads = [tile(p, 2 * a) for p in range(4)]
                    tiles = [heads[0]]
                    for p in range(4):
                        tiles.append(tile(p, 2 * a + 1))
                        end = pltpu.roll(spare[p], (4 * (p - a)) % 16, 0) if p != a else spare[p]
                        if p < 3:
                            end = jnp.where(row_half < 4 * p + 4, end, heads[p + 1])
                        tiles.append(jnp.where(row_half < 4 * p, heads[p], end) if p else end)
                    for i, value in enumerate(tiles):
                        wb[conv, a, 18 * spot + 9 * g + i, :, s * (C // 2) : (s + 1) * (C // 2)] = value.astype(BF16)
            return carry

        lax.fori_loop(0, 2, merge, 0)

    def weights_done(conv):
        copies = along_ha(conv)
        for j in range(N):
            copies += along_wa(conv, j) + along_ta(conv, j) + across(conv, j)
        for copy in copies:
            copy.wait_send()

    row_of = lax.broadcasted_iota(jnp.int32, (16, C), 0)

    top, bottom, left, right = ha > 0, ha < N - 1, wa > 0, wa < N - 1

    def put(lhs, t, h, v, before, after, flip):
        before = jnp.where(row_of == 0, before, pltpu.roll(v, 1, 0))
        after = jnp.where(row_of == 15, after, pltpu.roll(v, 15, 0))
        if flip:
            before, after = after, before
        lhs[t, h, :, 0:C] = before.astype(BF16)
        lhs[t, h, :, C : 2 * C] = v.astype(BF16)
        lhs[t, h, :, 2 * C : 3 * C] = after.astype(BF16)

    def fill_frame(lhs, t, frame, cell, side, corner, flip):
        edges = []
        for r, ok in ((0, left), (1, right)):
            ok = jnp.logical_and(ok, frame)
            mid = jnp.where(ok, side(r), 0.0)
            hi = jnp.where(jnp.logical_and(ok, top), corner(r, 0), 0.0)
            lo = jnp.where(jnp.logical_and(ok, bottom), corner(r, 1), 0.0)
            edges.append([hi] + [mid[h : h + 1] for h in range(8)] + [lo])
        for h in range(10):
            ok = frame
            if h == 0:
                ok = jnp.logical_and(ok, top)
            if h == 9:
                ok = jnp.logical_and(ok, bottom)
            put(lhs, t, h, jnp.where(ok, cell(h), 0.0), edges[0][h], edges[1][h], flip)

    def fill(lhs, refs, early, late, fn, flip):
        def body(t, carry):
            frame = jnp.logical_and(jnp.logical_or(t >= 2, early), jnp.logical_or(t < 2, late))
            fill_frame(
                lhs, t, frame,
                lambda h: fn(*[x[t, h] for x, _, _ in refs]),
                lambda r: fn(*[k[r, t] for _, k, _ in refs]),
                lambda r, b: fn(*[q[r, b, t] for _, _, q in refs]),
                flip,
            )
            return carry

        lax.fori_loop(0, 4, body, 0)

    def fill_narrow(lhs, field, flip):
        x, k, q, own = fields[field], cols[field], corners[field], OWN[field] // 2
        for t in range(4):
            w, u = t // 2, t % 2
            frame = True if w == own else (ta > 0 if own else ta < N - 1)
            fill_frame(
                lhs, t, frame,
                lambda h: x[t, h].astype(F32),
                lambda r: k[r, w].astype(F32)[8 * u : 8 * u + 8],
                lambda r, b: q[r, b, w].astype(F32)[u : u + 1],
                flip,
            )

    def convolve(lhs, conv, flip):
        total = None
        for a in range(3):
            for b in range(3):
                part = lhs[a : a + 2, b : b + 8].reshape(CELLS, 3 * C)
                if flip:
                    w = wb[conv, 2 - a, pl.ds(48 * (2 - b), 48)].reshape(3 * C, C)
                    out = None
                    for c in range(3):
                        one = lax.dot_general(
                            part[:, c * C : c * C + C], w[c * C : c * C + C, :],
                            (((1,), (1,)), ((), ())), preferred_element_type=F32,
                        )
                        out = one if out is None else out + one
                else:
                    w = wb[conv, a, pl.ds(48 * b, 48)].reshape(3 * C, C)
                    out = jnp.dot(part, w, preferred_element_type=F32)
                total = out if total is None else total + out
        return total.reshape(2, 8, 16, C)

    shard_stage(0, w_one)
    pl.semaphore_wait(barrier, count)
    start(along_ha(0))
    start(along_wa(0, 0))
    load_f.wait()
    reduce_send(0, 0, local_moments(fx, 2))
    halo_send(FEAT)
    shard_stage(1, w_two)
    start(along_ha(1))
    load_c.wait()
    nx[pl.ds(0, 2), pl.ds(1, 8)] = cx[...].astype(BF16)
    halo_send(COT)
    from_ha(0, 1)
    from_ha(0, 7)
    from_wa(0, 0)
    from_ha(0, 2)
    from_ha(0, 6)
    reduce_send(0, 1, merge_moments(0, 0))
    from_wa(0, 1)
    from_ha(0, 3)
    from_ha(0, 5)
    from_wa(0, 7)
    from_ha(0, 4)
    start(along_wa(1, 0))
    from_ha(1, 1)
    from_ta(0, 0)
    from_wa(0, 2)
    reduce_send(0, 2, merge_moments(0, 1))
    for j, k, m in ((1, 6, 7), (7, 3, 2), (2, 5, 6), (6, 4, 3)):
        from_ta(0, j)
        from_wa(0, k)
        from_ha(1, m)
    from_ha(1, 5)
    from_ha(1, 4)
    centre_1, inv_1 = finish_moments(merge_moments(0, 2))
    g1, b1, g2, b2 = gain_one[...], bias_one[...], gain_two[...], bias_two[...]
    halo_wait(FEAT)

    def act_one(v):
        inner = (v - centre_1) * inv_1 * g1 + b1
        return inner * sigmoid(inner)

    fill(lhs_a, [(fx, fk, fq)], ta > 0, True, act_one, False)
    for j in (0, 1, 7, 2):
        from_sibling(0, j)
    from_ta(0, 3)
    from_wa(1, 0)
    from_ta(0, 5)
    from_sibling(0, 6)
    from_ta(0, 4)
    from_wa(1, 1)
    from_sibling(0, 3)
    from_wa(1, 7)
    from_sibling(0, 5)
    from_sibling(0, 4)

    hx[pl.ds(0, 2), pl.ds(1, 8)] = convolve(lhs_a, 0, False)
    reduce_send(1, 0, local_moments(hx, 0))
    for j, k in ((2, 0), (6, 1), (3, 7)):
        from_wa(1, j)
        from_ta(1, k)
    reduce_send(1, 1, merge_moments(1, 0))
    for j, k in ((5, 2), (4, 6)):
        from_wa(1, j)
        from_ta(1, k)
    for j, k in ((3, 0), (5, 1), (4, 7)):
        from_ta(1, j)
        from_sibling(1, k)
    reduce_send(1, 2, merge_moments(1, 1))
    halo_send(HID)
    for j in (2, 6, 3, 5, 4):
        from_sibling(1, j)
    halo_wait(COT)
    fill_narrow(lhs_b, COT, True)
    gx[pl.ds(0, 2), pl.ds(1, 8)] = convolve(lhs_b, 1, True)
    halo_send(GRAD)
    centre_2, inv_2 = finish_moments(merge_moments(1, 2))

    def back_sums(field, own, grad, centre, inv, gain, bias):
        def body(i, carry):
            gain_sum, bias_sum = carry
            t, h = i // 8, i % 8
            unit = (field[own + t, 1 + h] - centre) * inv
            inner = unit * gain + bias
            s = sigmoid(inner)
            gi = grad(t, h) * s * (1.0 + inner * (1.0 - s))
            inner_grad[i] = gi
            unit_buf[i] = unit
            return gain_sum + gi * unit, bias_sum + gi

        zero = jnp.zeros((16, C), F32)
        sums = lax.fori_loop(0, 16, body, (zero, zero), unroll=8)
        return jnp.concatenate([jnp.sum(s, axis=0, keepdims=True) for s in sums], axis=0)

    reduce_send(2, 0, back_sums(hx, 0, lambda t, h: gx[t, 1 + h], centre_2, inv_2, g2, b2))

    def act_two(i, carry):
        inner = unit_buf[i] * g2 + b2
        mx[2 + i // 8, 1 + i % 8] = (inner * sigmoid(inner)).astype(BF16)
        return carry

    lax.fori_loop(0, 16, act_two, 0, unroll=4)
    halo_send(ACT)
    reduce_send(2, 1, merge_sums(2, 0))
    halo_wait(ACT)
    fill_narrow(lhs_a, ACT, False)
    reduce_send(2, 2, merge_sums(2, 1))
    block_out[...] = fx[pl.ds(2, 2), pl.ds(1, 8)] + convolve(lhs_a, 1, False)
    halo_wait(HID)
    halo_wait(GRAD)
    sums_2 = merge_sums(2, 2)
    norm_grads[2:4, :] = sums_2
    members = float(CELLS * N**3 * GROUP)
    both = group_sum(sums_2 * g2) * (1.0 / members)
    first_2, second_2 = both[1:2], both[0:1]

    def grad_hidden(v, g):
        unit = (v - centre_2) * inv_2
        inner = unit * g2 + b2
        s = sigmoid(inner)
        gi = g * s * (1.0 + inner * (1.0 - s))
        return (gi * g2 - first_2 - unit * second_2) * inv_2

    fill(lhs_b, [(hx, hk, hq), (gx, gk, gq)], True, ta < N - 1, grad_hidden, True)
    grad_act = convolve(lhs_b, 0, True)
    ga[...] = grad_act

    reduce_send(3, 0, back_sums(fx, 2, lambda t, h: ga[t, h], centre_1, inv_1, g1, b1))
    for field in (FEAT, COT, HID, ACT):
        halo_done(field)
    reduce_send(3, 1, merge_sums(3, 0))
    for conv in (0, 1):
        weights_done(conv)
    reduce_send(3, 2, merge_sums(3, 1))
    halo_done(GRAD)
    sums_1 = merge_sums(3, 2)
    norm_grads[0:2, :] = sums_1
    both = group_sum(sums_1 * g1) * (1.0 / members)
    first_1, second_1 = both[1:2], both[0:1]

    def last(i, carry):
        t, h = i // 8, i % 8
        field = (inner_grad[i] * g1 - first_1 - unit_buf[i] * second_1) * inv_1
        grad_input[t, h] = cx[t, h] + field
        return carry

    lax.fori_loop(0, 16, last, 0, unroll=8)
    for k in range(4):
        for s in range(3):
            for copy in reduce_copies(k, s):
                copy.wait_send()


def write_out(*refs):
    sems = refs[6]
    copies = [pltpu.make_async_copy(refs[i], refs[3 + i], sems.at[i]) for i in range(3)]
    for copy in copies:
        copy.start()
    for copy in copies:
        copy.wait()


def shards(features, cotangent, conv_one, conv_two, gain_one, bias_one, gain_two, bias_two):
    vmem = pl.BlockSpec(memory_space=pltpu.VMEM)
    anywhere = pl.BlockSpec(memory_space=pl.ANY)

    def buf(*shape, dtype=F32):
        return pltpu.VMEM(shape, dtype)

    scratch = (
        [buf(2, 8, 16, C)]
        + [buf(4, 10, 16, C)] * 3
        + [buf(4, 10, 16, C, dtype=BF16)] * 2
        + [buf(2, 4, 8, C)] * 3
        + [buf(2, 2, 16, C, dtype=BF16)] * 2
        + [buf(2, 2, 4, 1, C)] * 3
        + [buf(2, 2, 2, 16, C, dtype=BF16)] * 2
        + [buf(3, 2, 2, 8, C), buf(3, 2, 2, 2, 1, C)]
        + [buf(2, 2, 16, C, dtype=BF16), buf(2, 2, 2, 16, C, dtype=BF16)]
        + [buf(4, 10, 16, 3 * C, dtype=BF16)] * 2
        + [buf(2, N, 2, 2, 4, 7, 16, C // 2, dtype=BF16)]
        + [buf(2, 3, 144, 16, C, dtype=BF16)]
        + [buf(4, 3, 2, C), buf(4, 3, N, 2, C)]
        + [buf(16, 16, C)] * 2
        + [buf(2, 8, 16, C)]
        + [pltpu.SemaphoreType.DMA((2,))]
        + [pltpu.SemaphoreType.DMA((4, 3))] * 2
        + [pltpu.SemaphoreType.DMA((5, 27))] * 2
        + [pltpu.SemaphoreType.DMA((2, N))] * 4
        + [pltpu.SemaphoreType.DMA((2, N, 2))] * 2
        + [pltpu.SemaphoreType.DMA((2, N))] * 2
    )
    sizes = ((2, 8, 16, C), (2, 8, 16, C), (4, C))
    results = pl.pallas_call(
        kernel,
        out_shape=tuple(pltpu.VMEM(size, F32) for size in sizes),
        in_specs=[anywhere] * 2 + [vmem] * 6,
        out_specs=(vmem, vmem, vmem),
        scratch_shapes=scratch,
        compiler_params=pltpu.CompilerParams(
            collective_id=0, has_side_effects=True, vmem_limit_bytes=56 * 2**20
        ),
    )(
        features, cotangent, conv_one, conv_two,
        gain_one[None], bias_one[None], gain_two[None], bias_two[None],
    )
    return pl.pallas_call(
        write_out,
        out_shape=tuple(jax.ShapeDtypeStruct(size, F32) for size in sizes),
        in_specs=[vmem] * 3,
        out_specs=(anywhere,) * 3,
        scratch_shapes=[pltpu.SemaphoreType.DMA((3,))],
    )(*[pltpu.with_memory_space_constraint(r, pltpu.VMEM) for r in results])


def solution(mesh):
    return jax.shard_map(
        shards,
        mesh=mesh,
        in_specs=(
            P("ta", "ha", "wa", None),
            P("ta", "ha", "wa", None),
            P(None, ("ha", "wa"), None),
            P(None, ("ha", "wa"), None),
            P(),
            P(),
            P(),
            P(),
        ),
        out_specs=(P("ta", "ha", "wa", None), P("ta", "ha", "wa", None), P()),
        check_vma=False,
    )
```

```python
import functools

import jax
import jax.numpy as jnp
from jax import lax
from jax.experimental import pallas as pl
from jax.experimental.pallas import tpu as pltpu
from jax.sharding import PartitionSpec as P

AXES = ("ta", "ha", "wa")
N = 8
C = 256
GROUP = 8
NEAR = (1, 7, 2, 6, 3, 5, 4)
ORDER = ((0, 2, 1), (1, 2, 0), (1, 2, 0), (2, 1, 0))
EPS = 1e-06
CELLS = 256
MESH = pl.DeviceIdType.MESH
F32 = jnp.float32
BF16 = jnp.bfloat16

FEAT, HID, GRAD, COT, ACT = range(5)
NARROW = (COT, ACT)
OWN = {FEAT: 2, HID: 0, GRAD: 0, COT: 0, ACT: 2}


def sigmoid(v):
    return 1.0 / (1.0 + jnp.exp(-v))


def group_sum(v):
    lane = lax.broadcasted_iota(jnp.int32, v.shape, 1)
    for s in (1, 2, 4):
        up = pltpu.roll(v, s, 1)
        down = pltpu.roll(v, C - s, 1)
        v = v + jnp.where((lane & s) != 0, up, down)
    return v


def kernel(
    feat, cot, w_one, w_two, gain_one, bias_one, gain_two, bias_two,
    block_out, grad_input, norm_grads,
    cx, fx, hx, gx, nx, mx, fk, hk, gk, nk, mk, fq, hq, gq, nq, mq, ks, qs, ns, ms,
    lhs_a, lhs_b, shards_in, wb, stage, board, inner_grad, unit_buf, ga,
    local_sem, ar_s, ar_r, halo_s, halo_r, y_s, y_r, x_s, x_r, z_s, z_r, c_s, c_r,
):
    ta, ha, wa = (lax.axis_index(a) for a in AXES)
    me = (ta, ha, wa)
    core = lax.rem(wa, 2)
    sibling = (ta, ha, wa + 1 - 2 * core)
    fields = {FEAT: fx, HID: hx, GRAD: gx, COT: nx, ACT: mx}
    cols = {FEAT: fk, HID: hk, GRAD: gk, COT: nk, ACT: mk}
    corners = {FEAT: fq, HID: hq, GRAD: gq, COT: nq, ACT: mq}

    def along(axis, k):
        spot = list(me)
        spot[axis] = lax.rem(me[axis] + k, N)
        return tuple(spot)

    barrier = pltpu.get_barrier_semaphore()
    count = 0
    for axis in range(3):
        for k in range(1, N):
            pl.semaphore_signal(barrier, inc=1, device_id=along(axis, k), device_id_type=MESH)
            count += 1
    for dt in (-1, 0, 1):
        for dh in (-1, 0, 1):
            for dw in (-1, 0, 1):
                if abs(dt) + abs(dh) + abs(dw) >= 2:
                    spot = tuple(lax.rem(m + d + N, N) for m, d in zip(me, (dt, dh, dw)))
                    pl.semaphore_signal(barrier, inc=1, device_id=spot, device_id_type=MESH)
                    count += 1

    load_f = pltpu.make_async_copy(feat, fx.at[pl.ds(2, 2), pl.ds(1, 8)], local_sem.at[0])
    load_c = pltpu.make_async_copy(cot, cx, local_sem.at[1])
    load_f.start()
    load_c.start()

    def reduce_copies(k, s):
        axis = ORDER[k][s]
        return [
            pltpu.make_async_remote_copy(
                src_ref=stage.at[k, s],
                dst_ref=board.at[k, s, me[axis]],
                send_sem=ar_s.at[k, s],
                recv_sem=ar_r.at[k, s],
                device_id=along(axis, j),
                device_id_type=MESH,
            )
            for j in (4, 3, 5, 2, 6, 1, 7)
        ]

    def reduce_send(k, s, value):
        stage[k, s] = value
        board[k, s, me[ORDER[k][s]]] = value
        for copy in reduce_copies(k, s):
            copy.start()

    def reduce_get(k, s):
        seven = board.at[k, s, pl.ds(0, N - 1)]
        pltpu.make_async_copy(seven, seven, ar_r.at[k, s]).wait()
        return board[k, s]

    def merge_moments(k, s):
        got = reduce_get(k, s)
        cells = float(CELLS * N**s)
        means, squares = got[:, 0:1, :], got[:, 1:2, :]
        mean = jnp.sum(means, axis=0) * (1.0 / N)
        off = means - mean[None]
        square = jnp.sum(squares, axis=0) + cells * jnp.sum(off * off, axis=0)
        return jnp.concatenate([mean, square], axis=0)

    def merge_sums(k, s):
        return jnp.sum(reduce_get(k, s), axis=0)

    def local_moments(ref, own):
        v = ref[pl.ds(own, 2), pl.ds(1, 8)].reshape(CELLS, C)
        mean = jnp.sum(v, axis=0, keepdims=True) * (1.0 / CELLS)
        d = v - mean
        return jnp.concatenate([mean, jnp.sum(d * d, axis=0, keepdims=True)], axis=0)

    def finish_moments(pair):
        cells = float(CELLS * N**3)
        mean, square = pair[0:1], pair[1:2]
        centre = group_sum(mean) * (1.0 / GROUP)
        off = mean - centre
        spread = group_sum(square + cells * off * off) * (1.0 / (cells * GROUP))
        return centre, 1.0 / jnp.sqrt(spread + EPS)

    def halo_messages(field):
        own, x, k, q = OWN[field], fields[field], cols[field], corners[field]
        src_t = pl.ds(own, 2)
        narrow = field in NARROW
        for dt in (0, 1 if own else -1):
            dst_t = pl.ds(own - 2 * dt, 2)
            dst_k = (own - 2 * dt) // 2 if narrow else dst_t
            for dh in (0, -1, 1):
                for dw in (0, -1, 1):
                    if (dt, dh, dw) == (0, 0, 0):
                        continue
                    r, b = int(dw > 0), int(dh > 0)
                    if dh == 0 and dw == 0:
                        src, dst = x.at[src_t, pl.ds(1, 8)], x.at[dst_t, pl.ds(1, 8)]
                    elif dw == 0:
                        src, dst = x.at[src_t, 8 if b else 1], x.at[dst_t, 0 if b else 9]
                    elif dh == 0:
                        src = ns.at[field - COT, r] if narrow else ks.at[field, r]
                        dst = k.at[1 - r, dst_k]
                    else:
                        src = ms.at[field - COT, r, b] if narrow else qs.at[field, r, b]
                        dst = q.at[1 - r, 1 - b, dst_k]
                    spot = (ta + dt, ha + dh, wa + dw)
                    back = (ta - dt, ha - dh, wa - dw)
                    number = (dt + 1) * 9 + (dh + 1) * 3 + dw + 1
                    copy = pltpu.make_async_remote_copy(
                        src_ref=src, dst_ref=dst,
                        send_sem=halo_s.at[field, number], recv_sem=halo_r.at[field, number],
                        device_id=spot, device_id_type=MESH,
                    )
                    yield copy, inside(spot, (dt, dh, dw)), inside(back, (-dt, -dh, -dw))

    def inside(spot, delta):
        ok = None
        for v, d in zip(spot, delta):
            if d:
                one = v < N if d > 0 else v >= 0
                ok = one if ok is None else jnp.logical_and(ok, one)
        return ok

    def halo_send(field):
        own, x = OWN[field], fields[field]
        for r, w in ((0, 0), (1, 15)):
            if field in NARROW:
                ns[field - COT, r] = x[own : own + 2, 1:9, w, :].astype(F32).reshape(16, C).astype(BF16)
                for b, h in ((0, 1), (1, 8)):
                    pair = [x[own + t, h, w : w + 1, :].astype(F32) for t in range(2)]
                    ms[field - COT, r, b] = jnp.concatenate(pair + [jnp.zeros((14, C), F32)], axis=0).astype(BF16)
                continue
            for t in range(2):
                for h in range(8):
                    row = x[own + t, 1 + h, w : w + 1, :]
                    ks[field, r, t, h : h + 1, :] = row
                    if h in (0, 7):
                        qs[field, r, h // 7, t] = row
        for copy, goes, _ in halo_messages(field):
            pl.when(goes)(copy.start)

    def halo_wait(field):
        for copy, _, comes in halo_messages(field):
            pl.when(comes)(copy.wait_recv)

    def halo_done(field):
        for copy, goes, _ in halo_messages(field):
            pl.when(goes)(copy.wait_send)

    shift = 4 * lax.rem(wa, 4)
    half = lax.rem(ta, 2)
    column = lax.div(wa, 2)

    def block(j):
        return lax.rem(ha - j + N, N)

    row_half = lax.broadcasted_iota(jnp.int32, (16, C // 2), 0)

    def shard_stage(conv, ref):
        spare = None
        for a in range(3):
            rows = jnp.concatenate([ref[a].astype(F32), jnp.zeros((12, C), F32)], axis=0)
            rows = pltpu.roll(rows, shift, 0)
            rows = jnp.where(half == 0, rows[:, : C // 2], rows[:, C // 2 :])
            first, middle, end = rows[0:16], rows[16:32], rows[32:48]
            shards_in[conv, ha, core, half, column, 2 * a] = jnp.where(row_half >= shift, first, end).astype(BF16)
            shards_in[conv, ha, core, half, column, 2 * a + 1] = middle.astype(BF16)
            end = pltpu.roll(end, lax.rem(4 * a - shift + 16, 16), 0)
            spare = end if a == 0 else jnp.where(row_half >= 4 * a, end, spare)
        shards_in[conv, ha, core, half, column, 6] = spare.astype(BF16)

    def weight_copy(ref, sems, spot, device):
        return pltpu.make_async_remote_copy(
            src_ref=ref, dst_ref=ref, send_sem=sems[0].at[spot], recv_sem=sems[1].at[spot],
            device_id=device, device_id_type=MESH,
        )

    def along_ha(conv):
        ref = shards_in.at[conv, ha, core, half, column]
        return [weight_copy(ref, (y_s, y_r), (conv, j), along(1, j)) for j in NEAR]

    def along_wa(conv, j):
        ref = shards_in.at[conv, block(j), core, half, column]
        return [weight_copy(ref, (x_s, x_r), (conv, j), along(2, k)) for k in (2, 6, 4)]

    def along_ta(conv, j):
        ref = shards_in.at[conv, block(j), core, half]
        return [
            weight_copy(ref.at[pl.ds(0, 2)], (z_s, z_r), (conv, j, 0), along(0, 1)),
            weight_copy(ref.at[pl.ds(2, 2)], (z_s, z_r), (conv, j, 1), along(0, N - 1)),
        ]

    def across(conv, j):
        return [weight_copy(shards_in.at[conv, block(j), core], (c_s, c_r), (conv, j), sibling)]

    def start(copies):
        for copy in copies:
            copy.start()

    def arrived(ref, sem):
        pltpu.make_async_copy(ref, ref, sem).wait()

    def from_ha(conv, j):
        arrived(shards_in.at[conv, block(j), core, half, 0], y_r.at[conv, j])
        start(along_wa(conv, j))

    def from_wa(conv, j):
        arrived(shards_in.at[conv, block(j), core, half, pl.ds(0, 3)], x_r.at[conv, j])
        start(along_ta(conv, j))

    def from_ta(conv, j):
        ref = shards_in.at[conv, block(j), core, 1 - half]
        arrived(ref.at[pl.ds(0, 2)], z_r.at[conv, j, 0])
        arrived(ref.at[pl.ds(2, 2)], z_r.at[conv, j, 1])
        start(across(conv, j))

    def from_sibling(conv, j):
        arrived(shards_in.at[conv, block(j), 1 - core], c_r.at[conv, j])
        spot = block(j)

        def merge(g, carry):
            for s in range(2):
                def tile(p, i):
                    return shards_in[conv, spot, p % 2, s, 2 * g + p // 2, i].astype(F32)

                spare = [tile(p, 6) for p in range(4)]
                for a in range(3):
                    heads = [tile(p, 2 * a) for p in range(4)]
                    tiles = [heads[0]]
                    for p in range(4):
                        tiles.append(tile(p, 2 * a + 1))
                        end = pltpu.roll(spare[p], (4 * (p - a)) % 16, 0) if p != a else spare[p]
                        if p < 3:
                            end = jnp.where(row_half < 4 * p + 4, end, heads[p + 1])
                        tiles.append(jnp.where(row_half < 4 * p, heads[p], end) if p else end)
                    for i, value in enumerate(tiles):
                        wb[conv, a, 18 * spot + 9 * g + i, :, s * (C // 2) : (s + 1) * (C // 2)] = value.astype(BF16)
            return carry

        lax.fori_loop(0, 2, merge, 0)

    def weights_done(conv):
        copies = along_ha(conv)
        for j in range(N):
            copies += along_wa(conv, j) + along_ta(conv, j) + across(conv, j)
        for copy in copies:
            copy.wait_send()

    row_of = lax.broadcasted_iota(jnp.int32, (16, C), 0)

    top, bottom, left, right = ha > 0, ha < N - 1, wa > 0, wa < N - 1

    def put(lhs, t, h, v, before, after, flip):
        before = jnp.where(row_of == 0, before, pltpu.roll(v, 1, 0))
        after = jnp.where(row_of == 15, after, pltpu.roll(v, 15, 0))
        if flip:
            before, after = after, before
        lhs[t, h, :, 0:C] = before.astype(BF16)
        lhs[t, h, :, C : 2 * C] = v.astype(BF16)
        lhs[t, h, :, 2 * C : 3 * C] = after.astype(BF16)

    def fill_frame(lhs, t, frame, cell, side, corner, flip):
        edges = []
        for r, ok in ((0, left), (1, right)):
            ok = jnp.logical_and(ok, frame)
            mid = jnp.where(ok, side(r), 0.0)
            hi = jnp.where(jnp.logical_and(ok, top), corner(r, 0), 0.0)
            lo = jnp.where(jnp.logical_and(ok, bottom), corner(r, 1), 0.0)
            edges.append([hi] + [mid[h : h + 1] for h in range(8)] + [lo])
        for h in range(10):
            ok = frame
            if h == 0:
                ok = jnp.logical_and(ok, top)
            if h == 9:
                ok = jnp.logical_and(ok, bottom)
            put(lhs, t, h, jnp.where(ok, cell(h), 0.0), edges[0][h], edges[1][h], flip)

    def fill(lhs, refs, early, late, fn, flip):
        def body(t, carry):
            frame = jnp.logical_and(jnp.logical_or(t >= 2, early), jnp.logical_or(t < 2, late))
            fill_frame(
                lhs, t, frame,
                lambda h: fn(*[x[t, h] for x, _, _ in refs]),
                lambda r: fn(*[k[r, t] for _, k, _ in refs]),
                lambda r, b: fn(*[q[r, b, t] for _, _, q in refs]),
                flip,
            )
            return carry

        lax.fori_loop(0, 4, body, 0)

    def fill_narrow(lhs, field, flip):
        x, k, q, own = fields[field], cols[field], corners[field], OWN[field] // 2
        for t in range(4):
            w, u = t // 2, t % 2
            frame = True if w == own else (ta > 0 if own else ta < N - 1)
            fill_frame(
                lhs, t, frame,
                lambda h: x[t, h].astype(F32),
                lambda r: k[r, w].astype(F32)[8 * u : 8 * u + 8],
                lambda r, b: q[r, b, w].astype(F32)[u : u + 1],
                flip,
            )

    def convolve(lhs, conv, flip):
        total = None
        for a in range(3):
            for b in range(3):
                part = lhs[a : a + 2, b : b + 8].reshape(CELLS, 3 * C)
                if flip:
                    w = wb[conv, 2 - a, pl.ds(48 * (2 - b), 48)].reshape(3 * C, C)
                    out = None
                    for c in range(3):
                        one = lax.dot_general(
                            part[:, c * C : c * C + C], w[c * C : c * C + C, :],
                            (((1,), (1,)), ((), ())), preferred_element_type=F32,
                        )
                        out = one if out is None else out + one
                else:
                    w = wb[conv, a, pl.ds(48 * b, 48)].reshape(3 * C, C)
                    out = jnp.dot(part, w, preferred_element_type=F32)
                total = out if total is None else total + out
        return total.reshape(2, 8, 16, C)

    shard_stage(0, w_one)
    pl.semaphore_wait(barrier, count)
    start(along_ha(0))
    start(along_wa(0, 0))
    load_f.wait()
    reduce_send(0, 0, local_moments(fx, 2))
    halo_send(FEAT)
    shard_stage(1, w_two)
    start(along_ha(1))
    load_c.wait()
    nx[pl.ds(0, 2), pl.ds(1, 8)] = cx[...].astype(BF16)
    halo_send(COT)
    from_ha(0, 1)
    from_ha(0, 7)
    from_wa(0, 0)
    from_ha(0, 2)
    from_ha(0, 6)
    reduce_send(0, 1, merge_moments(0, 0))
    from_wa(0, 1)
    from_ha(0, 3)
    from_ha(0, 5)
    from_wa(0, 7)
    from_ha(0, 4)
    start(along_wa(1, 0))
    from_ha(1, 1)
    from_ta(0, 0)
    from_wa(0, 2)
    reduce_send(0, 2, merge_moments(0, 1))
    for j, k, m in ((1, 6, 7), (7, 3, 2), (2, 5, 6), (6, 4, 3)):
        from_ta(0, j)
        from_wa(0, k)
        from_ha(1, m)
    from_ha(1, 5)
    from_ha(1, 4)
    centre_1, inv_1 = finish_moments(merge_moments(0, 2))
    g1, b1, g2, b2 = gain_one[...], bias_one[...], gain_two[...], bias_two[...]
    halo_wait(FEAT)

    def act_one(v):
        inner = (v - centre_1) * inv_1 * g1 + b1
        return inner * sigmoid(inner)

    fill(lhs_a, [(fx, fk, fq)], ta > 0, True, act_one, False)
    for j in (0, 1, 7, 2):
        from_sibling(0, j)
    from_ta(0, 3)
    from_wa(1, 0)
    from_ta(0, 5)
    from_sibling(0, 6)
    from_ta(0, 4)
    from_wa(1, 1)
    from_sibling(0, 3)
    from_wa(1, 7)
    from_sibling(0, 5)
    from_sibling(0, 4)

    hx[pl.ds(0, 2), pl.ds(1, 8)] = convolve(lhs_a, 0, False)
    reduce_send(1, 0, local_moments(hx, 0))
    for j, k in ((2, 0), (6, 1), (3, 7)):
        from_wa(1, j)
        from_ta(1, k)
    reduce_send(1, 1, merge_moments(1, 0))
    for j, k in ((5, 2), (4, 6)):
        from_wa(1, j)
        from_ta(1, k)
    for j, k in ((3, 0), (5, 1), (4, 7)):
        from_ta(1, j)
        from_sibling(1, k)
    reduce_send(1, 2, merge_moments(1, 1))
    halo_send(HID)
    for j in (2, 6, 3, 5, 4):
        from_sibling(1, j)
    halo_wait(COT)
    fill_narrow(lhs_b, COT, True)
    gx[pl.ds(0, 2), pl.ds(1, 8)] = convolve(lhs_b, 1, True)
    halo_send(GRAD)
    centre_2, inv_2 = finish_moments(merge_moments(1, 2))

    def back_sums(field, own, grad, centre, inv, gain, bias):
        def body(i, carry):
            gain_sum, bias_sum = carry
            t, h = i // 8, i % 8
            unit = (field[own + t, 1 + h] - centre) * inv
            inner = unit * gain + bias
            s = sigmoid(inner)
            gi = grad(t, h) * s * (1.0 + inner * (1.0 - s))
            inner_grad[i] = gi
            unit_buf[i] = unit
            return gain_sum + gi * unit, bias_sum + gi

        zero = jnp.zeros((16, C), F32)
        sums = lax.fori_loop(0, 16, body, (zero, zero), unroll=8)
        return jnp.concatenate([jnp.sum(s, axis=0, keepdims=True) for s in sums], axis=0)

    reduce_send(2, 0, back_sums(hx, 0, lambda t, h: gx[t, 1 + h], centre_2, inv_2, g2, b2))

    def act_two(i, carry):
        inner = unit_buf[i] * g2 + b2
        mx[2 + i // 8, 1 + i % 8] = (inner * sigmoid(inner)).astype(BF16)
        return carry

    lax.fori_loop(0, 16, act_two, 0, unroll=4)
    halo_send(ACT)
    reduce_send(2, 1, merge_sums(2, 0))
    halo_wait(ACT)
    fill_narrow(lhs_a, ACT, False)
    reduce_send(2, 2, merge_sums(2, 1))
    block_out[...] = fx[pl.ds(2, 2), pl.ds(1, 8)] + convolve(lhs_a, 1, False)
    halo_wait(HID)
    halo_wait(GRAD)
    halo_done(HID)
    halo_done(GRAD)

    def scaled(h_ref, g_ref, spot):
        unit = (h_ref[spot] - centre_2) * inv_2
        inner = unit * g2 + b2
        s = sigmoid(inner)
        gi = g_ref[spot] * s * (1.0 + inner * (1.0 - s))
        h_ref[spot] = unit * inv_2
        g_ref[spot] = gi * g2 * inv_2

    def scale_frame(t, carry):
        for h in range(10):
            scaled(hx, gx, (t, h))
        for r in range(2):
            scaled(hk, gk, (r, t))
            for b in range(2):
                scaled(hq, gq, (r, b, t))
        return carry

    lax.fori_loop(0, 4, scale_frame, 0)
    sums_2 = merge_sums(2, 2)
    norm_grads[2:4, :] = sums_2
    members = float(CELLS * N**3 * GROUP)
    both = group_sum(sums_2 * g2) * (1.0 / members)
    first_2, second_2 = both[1:2], both[0:1]

    def grad_hidden(u, g):
        return g - first_2 * inv_2 - u * second_2

    fill(lhs_b, [(hx, hk, hq), (gx, gk, gq)], True, ta < N - 1, grad_hidden, True)
    grad_act = convolve(lhs_b, 0, True)
    ga[...] = grad_act

    reduce_send(3, 0, back_sums(fx, 2, lambda t, h: ga[t, h], centre_1, inv_1, g1, b1))
    for field in (FEAT, COT, ACT):
        halo_done(field)
    reduce_send(3, 1, merge_sums(3, 0))
    for conv in (0, 1):
        weights_done(conv)
    reduce_send(3, 2, merge_sums(3, 1))
    sums_1 = merge_sums(3, 2)
    norm_grads[0:2, :] = sums_1
    both = group_sum(sums_1 * g1) * (1.0 / members)
    first_1, second_1 = both[1:2], both[0:1]

    def last(i, carry):
        t, h = i // 8, i % 8
        field = (inner_grad[i] * g1 - first_1 - unit_buf[i] * second_1) * inv_1
        grad_input[t, h] = cx[t, h] + field
        return carry

    lax.fori_loop(0, 16, last, 0, unroll=8)
    for k in range(4):
        for s in range(3):
            for copy in reduce_copies(k, s):
                copy.wait_send()


def write_out(*refs):
    sems = refs[6]
    copies = [pltpu.make_async_copy(refs[i], refs[3 + i], sems.at[i]) for i in range(3)]
    for copy in copies:
        copy.start()
    for copy in copies:
        copy.wait()


def shards(features, cotangent, conv_one, conv_two, gain_one, bias_one, gain_two, bias_two):
    vmem = pl.BlockSpec(memory_space=pltpu.VMEM)
    anywhere = pl.BlockSpec(memory_space=pl.ANY)

    def buf(*shape, dtype=F32):
        return pltpu.VMEM(shape, dtype)

    scratch = (
        [buf(2, 8, 16, C)]
        + [buf(4, 10, 16, C)] * 3
        + [buf(4, 10, 16, C, dtype=BF16)] * 2
        + [buf(2, 4, 8, C)] * 3
        + [buf(2, 2, 16, C, dtype=BF16)] * 2
        + [buf(2, 2, 4, 1, C)] * 3
        + [buf(2, 2, 2, 16, C, dtype=BF16)] * 2
        + [buf(3, 2, 2, 8, C), buf(3, 2, 2, 2, 1, C)]
        + [buf(2, 2, 16, C, dtype=BF16), buf(2, 2, 2, 16, C, dtype=BF16)]
        + [buf(4, 10, 16, 3 * C, dtype=BF16)] * 2
        + [buf(2, N, 2, 2, 4, 7, 16, C // 2, dtype=BF16)]
        + [buf(2, 3, 144, 16, C, dtype=BF16)]
        + [buf(4, 3, 2, C), buf(4, 3, N, 2, C)]
        + [buf(16, 16, C)] * 2
        + [buf(2, 8, 16, C)]
        + [pltpu.SemaphoreType.DMA((2,))]
        + [pltpu.SemaphoreType.DMA((4, 3))] * 2
        + [pltpu.SemaphoreType.DMA((5, 27))] * 2
        + [pltpu.SemaphoreType.DMA((2, N))] * 4
        + [pltpu.SemaphoreType.DMA((2, N, 2))] * 2
        + [pltpu.SemaphoreType.DMA((2, N))] * 2
    )
    sizes = ((2, 8, 16, C), (2, 8, 16, C), (4, C))
    results = pl.pallas_call(
        kernel,
        out_shape=tuple(pltpu.VMEM(size, F32) for size in sizes),
        in_specs=[anywhere] * 2 + [vmem] * 6,
        out_specs=(vmem, vmem, vmem),
        scratch_shapes=scratch,
        compiler_params=pltpu.CompilerParams(
            collective_id=0, has_side_effects=True, vmem_limit_bytes=56 * 2**20
        ),
    )(
        features, cotangent, conv_one, conv_two,
        gain_one[None], bias_one[None], gain_two[None], bias_two[None],
    )
    return pl.pallas_call(
        write_out,
        out_shape=tuple(jax.ShapeDtypeStruct(size, F32) for size in sizes),
        in_specs=[vmem] * 3,
        out_specs=(anywhere,) * 3,
        scratch_shapes=[pltpu.SemaphoreType.DMA((3,))],
    )(*[pltpu.with_memory_space_constraint(r, pltpu.VMEM) for r in results])


def solution(mesh):
    return jax.shard_map(
        shards,
        mesh=mesh,
        in_specs=(
            P("ta", "ha", "wa", None),
            P("ta", "ha", "wa", None),
            P(None, ("ha", "wa"), None),
            P(None, ("ha", "wa"), None),
            P(),
            P(),
            P(),
            P(),
        ),
        out_specs=(P("ta", "ha", "wa", None), P("ta", "ha", "wa", None), P()),
        check_vma=False,
    )
```
